32 devices in a mesh: slab: 32 (over z, y, x, core).
Axes of the slice: x: 2, y: 2, z: 4, core: 2. Of those that a mesh axis runs over, the one named last changes fastest.
Arguments:
- coords: float32 [3, 65536], P(None, 'slab'), may hold values from -18 to 256, as said below
- charges: float32 [65536], P('slab'), may hold values from -3.6 to 3.6
- radii: float32 [65536], P('slab'), may hold values from 1.2 to 2
- screens: float32 [65536], P('slab'), may hold values from 0.6 to 0.9
- tile_lists: int32 [512, 8], P('slab'), may hold values from 0 to 79, as said below
- tile_counts: int32 [512], P('slab'), may hold values from 1 to 8, as said below
- slab_fill: int32 [32], P('slab'), may hold values from 1921 to 2048
Outputs:
- born_radii: float32 [65536], P('slab')
- energy: float32 [65536], P('slab')
- total: float32 [], replicated
The draws below stay inside these ranges and needn't reach their ends.
Inputs may be any that keep to these rules, and one draw needn't show every extreme that they name: `coords`: x and y lie within 18 of the fibre axis; z of atoms of slab s lies in [8 s, 8 s + 8]. `tile_lists`: entry 0 of tile g's list is its own tile, 32 + g % 16; the entries of a row are distinct; listed tiles lie in slabs that exist (the fibre does not close) and within 32 window tiles of the own tile. `tile_counts`: every slab has a tile whose count is 8.
All inputs are finite; a program needn't handle non-finite values.
Results may differ from the reference program's by a relative error of at most 0.0003.
Values sent between devices are 32-bit elements; how exact they have to be, the bound alone decides.
A program may use at most 64 MiB of HBM per device.

```python
import math
import jax
import jax.numpy as jnp
from jax import lax

ATOM_DEV = 2048
MAXT = 8
TPD = 16
SLABS = 32
ATOMS = 65536


def draw_coords(key, part):
    key_list = jax.random.split(jax.random.fold_in(key, 11), 3)
    slot_ids = jnp.arange(ATOMS)
    slab_place = (slot_ids // ATOM_DEV).astype(jnp.float32)
    within = (slot_ids % ATOM_DEV).astype(jnp.float32)
    along = jax.random.uniform(key_list[0], (ATOMS,), jnp.float32)
    spread_draw = jax.random.uniform(key_list[1], (ATOMS,), jnp.float32)
    turning = jax.random.uniform(key_list[2], (ATOMS,), jnp.float32, -math.pi, math.pi)
    radial = 18.0 * jnp.sqrt(spread_draw)
    height = 8.0 * (slab_place + (within + along) / ATOM_DEV)
    height = jnp.clip(height, 8.0 * slab_place, 8.0 * slab_place + 8.0)
    return jnp.stack([radial * jnp.cos(turning), radial * jnp.sin(turning), height]).astype(jnp.float32)


def draw_charges(key, part):
    slab_place = (jnp.arange(ATOMS) // ATOM_DEV).astype(jnp.float32) / (SLABS - 1)
    values = jnp.clip(jax.random.normal(jax.random.fold_in(key, 12), (ATOMS,), jnp.float32), -3.0, 3.0)
    factor = 0.4 * (1.0 + 2.0 * slab_place)
    return (values * factor).astype(jnp.float32)


def draw_radii(key, part):
    key_list = jax.random.split(jax.random.fold_in(key, 15), 3)
    upper = jax.random.randint(key_list[0], (ATOMS,), 0, 2, jnp.int32) == 1
    high = jax.random.uniform(key_list[1], (ATOMS,), jnp.float32, 1.85, 2.0)
    broad = jax.random.uniform(key_list[2], (ATOMS,), jnp.float32, 1.2, 2.0)
    return jnp.where(upper, high, broad).astype(jnp.float32)


def draw_screens(key, part):
    key_list = jax.random.split(jax.random.fold_in(key, 16), 3)
    upper = jax.random.randint(key_list[0], (ATOMS,), 0, 2, jnp.int32) == 1
    high = jax.random.uniform(key_list[1], (ATOMS,), jnp.float32, 0.84, 0.9)
    broad = jax.random.uniform(key_list[2], (ATOMS,), jnp.float32, 0.6, 0.9)
    return jnp.where(upper, high, broad).astype(jnp.float32)


def draw_tile_lists(key, part):
    total_tiles = SLABS * TPD
    window_tiles = 5 * TPD
    tile_ids = jnp.arange(total_tiles, dtype=jnp.int32)
    slab_ids = tile_ids // TPD
    own_tiles = 2 * TPD + tile_ids % TPD
    window_ids = jnp.arange(window_tiles, dtype=jnp.int32)
    slab_offset = window_ids // TPD - 2
    target_slab = slab_ids[:, None] + slab_offset[None, :]
    separation = jnp.abs(window_ids[None, :] - own_tiles[:, None])
    usable = (target_slab >= 0) & (target_slab < SLABS) & (separation > 0) & (separation <= 2 * TPD)
    score = jax.random.randint(jax.random.fold_in(key, 13), (total_tiles, window_tiles), 0, 65536, jnp.int32)
    ranked = jnp.where(usable, score * 1024 + window_ids[None, :], -1 - window_ids[None, :])
    chosen = lax.top_k(ranked, MAXT - 1)[1].astype(jnp.int32)
    return jnp.concatenate([own_tiles[:, None], chosen], axis=1).astype(jnp.int32)


def draw_tile_counts(key, part):
    key_list = jax.random.split(jax.random.fold_in(key, 14), 3)
    ceiling = jax.random.randint(key_list[0], (SLABS,), max(1, MAXT // 2), MAXT + 1, jnp.int32)
    per_tile = jnp.repeat(ceiling, TPD)
    floor_tile = jnp.maximum(per_tile // 2, 1)
    counts = jax.random.randint(key_list[1], (SLABS * TPD,), floor_tile, per_tile + 1, jnp.int32)
    heaviest = jax.random.randint(key_list[2], (SLABS,), 0, TPD, jnp.int32)
    position = jnp.arange(SLABS * TPD, dtype=jnp.int32) % TPD
    return jnp.where(position == jnp.repeat(heaviest, TPD), MAXT, counts).astype(jnp.int32)


def plant(drawn, own_key, smallest, high):
    longest = drawn.shape.index(max(drawn.shape))
    spots = []
    for shift in (0, 1):
        where = [jax.random.randint(jax.random.fold_in(own_key, axis), (), 0, length) for axis, length in enumerate(drawn.shape)]
        where[longest] = (where[longest] + shift) % drawn.shape[longest]
        spots.append(tuple(where))
    return drawn.at[spots[0]].set(smallest).at[spots[1]].set(high)


def setup_inputs(seed: int = 0) -> dict:
    seeds = jax.random.split(jax.random.key(seed), 8)
    return {
        "coords": draw_coords(jax.random.fold_in(seeds[7], 71), 0),
        "charges": draw_charges(jax.random.fold_in(seeds[7], 71), 0),
        "radii": draw_radii(jax.random.fold_in(seeds[7], 71), 0),
        "screens": draw_screens(jax.random.fold_in(seeds[7], 71), 0),
        "tile_lists": draw_tile_lists(jax.random.fold_in(seeds[7], 71), 0),
        "tile_counts": draw_tile_counts(jax.random.fold_in(seeds[7], 71), 0),
        "slab_fill": plant(jax.random.randint(seeds[6], (SLABS,), ATOM_DEV - 127, ATOM_DEV + 1), jax.random.fold_in(seeds[6], 1), ATOM_DEV - 127, ATOM_DEV).astype(jnp.int32),
    }


OFFSET = 0.09
SOFTEN = 1.0
group_tiles = 4

def pair_geometry(own_atoms, partner_atoms, list_block, count_block, first_block):
    squared = jnp.zeros((own_atoms.shape[1], 128, partner_atoms.shape[2], 128), jnp.float32)
    for component in range(3):
        offsets = own_atoms[component][:, :, None, None] - partner_atoms[component][:, None, :, :]
        squared = squared + offsets * offsets
    slot_ids = jnp.arange(partner_atoms.shape[2], dtype=jnp.int32)
    used_slot = (slot_ids[None, :] < count_block[:, None])[:, None, :, None]
    partner_mask = used_slot & (partner_atoms[6] > 0.5)[:, None, :, :] & (own_atoms[6] > 0.5)[:, :, None, None]
    lanes = jnp.arange(128, dtype=jnp.int32)
    own_ids = first_block[:, None] * 128 + lanes[None, :]
    partner_ids = list_block[:, :, None] * 128 + lanes[None, None, :]
    distinct = own_ids[:, :, None, None] != partner_ids[:, None, :, :]
    return (squared, partner_mask, distinct)

def born_block(own_atoms, partner_atoms, list_block, count_block, first_block):
    squared, partner_mask, distinct = pair_geometry(own_atoms, partner_atoms, list_block, count_block, first_block)
    own_live = own_atoms[6] > 0.5
    radius_own = jnp.where(own_live, own_atoms[4], 1.5)
    radius_partner = jnp.where(partner_atoms[6] > 0.5, partner_atoms[4], 1.5)[:, None, :, :]
    screen_partner = jnp.where(partner_atoms[6] > 0.5, partner_atoms[5], 0.8)[:, None, :, :]
    offset_radius = (radius_own - OFFSET)[:, :, None, None]
    scaled_radius = screen_partner * (radius_partner - OFFSET)
    distance = jnp.sqrt(squared + SOFTEN)
    upper_end = distance + scaled_radius
    lower_end = jnp.maximum(offset_radius, jnp.abs(distance - scaled_radius))
    pair_term = 0.5 * (1.0 / lower_end - 1.0 / upper_end + 0.25 * (distance - scaled_radius * scaled_radius / distance) * (1.0 / (upper_end * upper_end) - 1.0 / (lower_end * lower_end)) + 0.5 * jnp.log(lower_end / upper_end) / distance)
    pair_term = pair_term + jnp.where(offset_radius < scaled_radius - distance, 2.0 * (1.0 / offset_radius - 1.0 / lower_end), 0.0)
    counted = partner_mask & distinct & (offset_radius < upper_end)
    integral = lax.optimization_barrier(jnp.sum(jnp.where(counted, pair_term, 0.0), axis=(2, 3)))
    inner_radius = radius_own - OFFSET
    psi_value = integral * inner_radius
    bending = jnp.tanh(psi_value - 0.8 * psi_value * psi_value + 4.85 * psi_value * psi_value * psi_value)
    result = 1.0 / (1.0 / inner_radius - bending / radius_own)
    return jnp.where(own_live, result, 0.0)

def energy_block(own_atoms, partner_atoms, radius_own, radius_partner, list_block, count_block, first_block):
    squared, partner_mask, distinct = pair_geometry(own_atoms, partner_atoms, list_block, count_block, first_block)
    own_live = own_atoms[6] > 0.5
    born_own = jnp.where(own_live, radius_own, 1.0)[:, :, None, None]
    born_partner = jnp.where(partner_atoms[6] > 0.5, radius_partner, 1.0)[:, None, :, :]
    product = born_own * born_partner
    screened = jnp.sqrt(squared + product * jnp.exp(-squared / (4.0 * product)))
    pair_term = jnp.where(partner_mask, partner_atoms[3][:, None, :, :] / screened, 0.0)
    result = -0.5 * own_atoms[3] * lax.optimization_barrier(jnp.sum(pair_term, axis=(2, 3)))
    return jnp.where(own_live, result, 0.0)

def tile_setup(window, lists, counts):
    width = window.shape[1]
    tiles = width // 640
    blocks = tiles // group_tiles
    tiled = window.reshape(window.shape[0], width // 128, 128)
    own_atoms = tiled[:, 2 * tiles:3 * tiles].reshape(window.shape[0], blocks, group_tiles, 128).transpose(1, 0, 2, 3)
    list_groups = lists.reshape(blocks, group_tiles, lists.shape[1])
    count_groups = counts.reshape(blocks, group_tiles)
    first_tiles = (2 * tiles + jnp.arange(tiles, dtype=jnp.int32)).reshape(blocks, group_tiles)
    return (tiled, own_atoms, list_groups, count_groups, first_tiles)

def slab_born(window, lists, counts):
    tiled, own_atoms, list_groups, count_groups, first_tiles = tile_setup(window, lists, counts)

    def one_block(inputs):
        own_block, list_block, count_block, first_block = inputs
        partner_atoms = jnp.take(tiled, list_block, axis=1)
        return born_block(own_block, partner_atoms, list_block, count_block, first_block)
    result = lax.map(one_block, (own_atoms, list_groups, count_groups, first_tiles))
    return result.reshape(-1)

def slab_energy(window, radius_window, lists, counts):
    tiled, own_atoms, list_groups, count_groups, first_tiles = tile_setup(window, lists, counts)
    radius_tiled = radius_window.reshape(-1, 128)
    tiles = radius_tiled.shape[0] // 5
    radius_groups = radius_tiled[2 * tiles:3 * tiles].reshape(-1, group_tiles, 128)

    def one_block(inputs):
        own_block, radius_block, list_block, count_block, first_block = inputs
        partner_atoms = jnp.take(tiled, list_block, axis=1)
        partner_radii = jnp.take(radius_tiled, list_block, axis=0)
        return energy_block(own_block, partner_atoms, radius_block, partner_radii, list_block, count_block, first_block)
    result = lax.map(one_block, (own_atoms, radius_groups, list_groups, count_groups, first_tiles))
    return result.reshape(-1)

def reference(coords, charges, radii, screens, tile_lists, tile_counts, slab_fill):
    slot_index = jnp.arange(ATOMS, dtype=jnp.int32)
    live_flag = (slot_index % ATOM_DEV < slab_fill[slot_index // ATOM_DEV]).astype(jnp.float32)
    packed = jnp.concatenate([coords, charges[None], radii[None], screens[None], live_flag[None]], axis=0)
    padded = jnp.pad(packed, ((0, 0), (2 * ATOM_DEV, 2 * ATOM_DEV)))
    lists = tile_lists.reshape(SLABS, TPD, MAXT)
    counts = tile_counts.reshape(SLABS, TPD)
    slab_ids = jnp.arange(SLABS, dtype=jnp.int32)

    def born_of(inputs):
        slab_id, slab_lists, slab_counts = inputs
        start = (slab_id * ATOM_DEV).astype(jnp.int32)
        window = lax.dynamic_slice(padded, (jnp.zeros((), jnp.int32), start), (7, 5 * ATOM_DEV))
        return slab_born(window, slab_lists, slab_counts)
    born_radii = lax.map(born_of, (slab_ids, lists, counts)).reshape(ATOMS)
    radius_padded = jnp.pad(born_radii, (2 * ATOM_DEV, 2 * ATOM_DEV))

    def energy_of(inputs):
        slab_id, slab_lists, slab_counts = inputs
        start = (slab_id * ATOM_DEV).astype(jnp.int32)
        window = lax.dynamic_slice(padded, (jnp.zeros((), jnp.int32), start), (7, 5 * ATOM_DEV))
        radius_window = lax.dynamic_slice(radius_padded, (start,), (5 * ATOM_DEV,))
        return slab_energy(window, radius_window, slab_lists, slab_counts)
    energy = lax.map(energy_of, (slab_ids, lists, counts)).reshape(ATOMS)
    return (born_radii, energy, jnp.sum(energy))
```

```python
import functools

import jax
import jax.numpy as jnp
from jax import lax
from jax.experimental import pallas as pl
from jax.experimental.pallas import tpu as pltpu
from jax.sharding import PartitionSpec as P

OFFSET = 0.09
SOFTEN = 1.0
LOG2E = 1.4426950408889634
MESH = pl.DeviceIdType.MESH
SHIFTS = (1, -1, 2, -2)
LANES = 128
ROWS = 8


def squared_distance(own, partner):
    dx = own[0] - partner[0]
    dy = own[1] - partner[1]
    dz = own[2] - partner[2]
    return dx * dx + dy * dy + dz * dz


def born_parts(squared, offset_own, scaled, diagonal=None):
    soft = squared + SOFTEN
    inverse = lax.rsqrt(soft)
    distance = soft * inverse
    upper = distance + scaled
    reach = distance - scaled
    inner = jnp.maximum(offset_own, scaled - distance)
    lower = jnp.minimum(jnp.maximum(inner, reach), upper)
    both = pl.reciprocal(upper * lower, approx=True)
    over_lower = upper * both
    over_upper = lower * both
    apart = over_lower - over_upper
    bend = distance - scaled * scaled * inverse
    first = apart * (4.0 - bend * (over_lower + over_upper))
    second = inverse * jnp.log(lower * over_upper)
    third = (inner - offset_own) * over_lower
    if diagonal is not None:
        first = jnp.where(diagonal, 0.0, first)
        second = jnp.where(diagonal, 0.0, second)
        third = jnp.where(diagonal, 0.0, third)
    return first, second, third


def energy_part(squared, born_own, rate_own, born_partner, over_partner, charge_partner):
    spread = jnp.exp2(squared * (rate_own * over_partner))
    return charge_partner * lax.rsqrt(squared + (born_own * born_partner) * spread)


def kernel(
    count,
    lists,
    counts,
    fill,
    coords,
    charges,
    radii,
    screens,
    born_out,
    energy_out,
    total_out,
    window,
    born_window,
    total_window,
    columns,
    born_columns,
    partners,
    sums,
    result,
    window_send,
    window_recv,
    born_send,
    born_recv,
    total_send,
    total_recv,
):
    me = lax.axis_index("slab")
    tiles = charges.shape[0]
    width = lists.shape[1]
    steps = LANES // ROWS

    barrier = pltpu.get_barrier_semaphore()

    def greet(step, carry):
        pl.semaphore_signal(
            barrier, inc=1, device_id=(lax.rem(me + step, count),), device_id_type=MESH
        )
        return carry

    lax.fori_loop(1, count, greet, 0)

    slots = lax.broadcasted_iota(jnp.int32, (tiles, LANES), 0) * LANES
    slots = slots + lax.broadcasted_iota(jnp.int32, (tiles, LANES), 1)
    live = slots < fill[0]
    offset_own = jnp.where(live, radii[...] - OFFSET, 1.5 - OFFSET)
    home = pl.ds(2 * tiles, tiles)
    for component in range(3):
        for tile in range(tiles):
            window[component, 2 * tiles + tile : 2 * tiles + tile + 1, :] = coords[
                component : component + 1, tile * LANES : (tile + 1) * LANES
            ]
    window[3, home, :] = jnp.where(live, charges[...], 0.0)
    window[4, home, :] = jnp.where(live, screens[...] * (radii[...] - OFFSET), 0.0)
    result[...] = offset_own

    def there(shift):
        return jnp.logical_and(me + shift >= 0, me + shift < count)

    def send(buffer, sems_out, sems_in, place, shift):
        def view(spot):
            rows = pl.ds(spot * tiles, tiles)
            return buffer.at[:, rows, :] if len(buffer.shape) == 3 else buffer.at[rows, :]

        return pltpu.make_async_remote_copy(
            src_ref=view(2),
            dst_ref=view(2 - shift),
            send_sem=sems_out.at[place],
            recv_sem=sems_in.at[place],
            device_id=(me + shift,),
            device_id_type=MESH,
        )

    def send_all(buffer, sems_out, sems_in):
        for place, shift in enumerate(SHIFTS):
            copy = send(buffer, sems_out, sems_in, place, shift)
            pl.when(there(shift))(copy.start)

    def wait_all(buffer, sems_out, sems_in):
        for place, shift in enumerate(SHIFTS):
            copy = send(buffer, sems_out, sems_in, place, shift)
            pl.when(there(shift))(copy.wait_send)
            pl.when(there(-shift))(copy.wait_recv)

    for shift in SHIFTS:

        @pl.when(jnp.logical_not(there(-shift)))
        def _():
            rows = pl.ds((2 - shift) * tiles, tiles)
            window[:, rows, :] = jnp.zeros((5, tiles, LANES), jnp.float32)
            born_window[rows, :] = jnp.ones((tiles, LANES), jnp.float32)

    pl.semaphore_wait(barrier, count - 1)
    send_all(window, window_send, window_recv)

    def diagonal_of(row):
        own_slot = lax.broadcasted_iota(jnp.int32, (ROWS, LANES), 0) + row
        return own_slot == lax.broadcasted_iota(jnp.int32, (ROWS, LANES), 1)

    def row_of(buffer, index):
        return jnp.broadcast_to(buffer[pl.ds(index, 1), :], (ROWS, LANES))

    def spread_columns(rows):
        return [jnp.broadcast_to(row, (LANES, LANES)).T for row in rows]

    def born_near(tile, carry):
        own_rows = [window[c, pl.ds(2 * tiles + tile, 1), :] for c in range(3)]
        own_rows.append(result[pl.ds(tile, 1), :])
        for place, block in enumerate(spread_columns(own_rows)):
            columns[tile, place] = block
        partner = [row_of(window.at[c], 2 * tiles + tile) for c in (0, 1, 2, 4)]
        for step in range(steps):
            rows = pl.ds(step * ROWS, ROWS)
            own = [columns[tile, c, rows, :] for c in range(4)]
            terms = born_parts(
                squared_distance(own, partner), own[3], partner[3], diagonal_of(step * ROWS)
            )
            for place, term in enumerate(terms):
                sums[tile, place, rows, :] = term
        return carry

    lax.fori_loop(0, tiles, born_near, 0)
    wait_all(window, window_send, window_recv)

    def gather_partner(tile, entry):
        index = lists[tile, entry]
        used = entry < counts[tile]
        for place in range(5):
            row = row_of(window.at[place], index)
            partners[entry, place] = jnp.where(used, row, 0.0)
        return index, used

    def born_far(tile, carry):
        for entry in range(1, width):
            gather_partner(tile, entry)

        def one_step(step, inner):
            rows = pl.ds(pl.multiple_of(step * ROWS, ROWS), ROWS)
            own = [columns[tile, c, rows, :] for c in range(4)]
            totals = [sums[tile, c, rows, :] for c in range(3)]
            for entry in range(1, width):
                partner = [partners[entry, c] for c in (0, 1, 2, 4)]
                terms = born_parts(squared_distance(own, partner), own[3], partner[3])
                totals = [old + term for old, term in zip(totals, terms)]
            sums[tile, 0, rows, :] = 0.125 * totals[0] + 0.25 * totals[1] + 2.0 / own[3] * totals[2]
            return inner

        lax.fori_loop(0, steps, one_step, 0, unroll=2)
        born_out[pl.ds(tile, 1), :] = jnp.sum(sums[tile, 0].T, axis=0, keepdims=True)
        return carry

    lax.fori_loop(0, tiles, born_far, 0)

    radius_own = jnp.where(live, radii[...], 1.5)
    psi = born_out[...] * offset_own
    bending = jnp.tanh(psi - 0.8 * psi * psi + 4.85 * psi * psi * psi)
    born = 1.0 / (1.0 / offset_own - bending / radius_own)
    born_out[...] = jnp.where(live, born, 0.0)
    born_window[home, :] = jnp.where(live, born, 1.0)
    send_all(born_window, born_send, born_recv)

    def energy_near(tile, carry):
        own_born = born_window[pl.ds(2 * tiles + tile, 1), :]
        blocks = spread_columns([own_born, (-0.25 * LOG2E) / own_born])
        for place, block in enumerate(blocks):
            born_columns[tile, place] = block
        partner = [row_of(window.at[c], 2 * tiles + tile) for c in range(4)]
        partner_born = row_of(born_window, 2 * tiles + tile)
        over_partner = 1.0 / partner_born
        for step in range(steps):
            rows = pl.ds(step * ROWS, ROWS)
            own = [columns[tile, c, rows, :] for c in range(3)]
            sums[tile, 0, rows, :] = energy_part(
                squared_distance(own, partner),
                born_columns[tile, 0, rows, :],
                born_columns[tile, 1, rows, :],
                partner_born,
                over_partner,
                partner[3],
            )
        return carry

    lax.fori_loop(0, tiles, energy_near, 0)
    wait_all(born_window, born_send, born_recv)

    def energy_far(tile, carry):
        for entry in range(1, width):
            index, used = gather_partner(tile, entry)
            row = jnp.where(used, row_of(born_window, index), 1.0)
            partners[entry, 4] = row
            partners[entry, 5] = 1.0 / row

        def one_step(step, inner):
            rows = pl.ds(pl.multiple_of(step * ROWS, ROWS), ROWS)
            own = [columns[tile, c, rows, :] for c in range(3)]
            own_born = [born_columns[tile, c, rows, :] for c in range(2)]
            total = sums[tile, 0, rows, :]
            for entry in range(1, width):
                partner = [partners[entry, c] for c in range(6)]
                total = total + energy_part(
                    squared_distance(own, partner), *own_born, partner[4], partner[5], partner[3]
                )
            sums[tile, 0, rows, :] = total
            return inner

        lax.fori_loop(0, steps, one_step, 0, unroll=2)
        result[pl.ds(tile, 1), :] = jnp.sum(sums[tile, 0].T, axis=0, keepdims=True)
        return carry

    lax.fori_loop(0, tiles, energy_far, 0)

    energy = -0.5 * window[3, home, :] * result[...]
    energy_out[...] = energy
    total_window[pl.ds(me, 1), :] = jnp.sum(energy, axis=0, keepdims=True)

    def total_copy(step):
        mine = total_window.at[pl.ds(me, 1), :]
        return pltpu.make_async_remote_copy(
            src_ref=mine,
            dst_ref=mine,
            send_sem=total_send.at[step],
            recv_sem=total_recv.at[step],
            device_id=(lax.rem(me + step, count),),
            device_id_type=MESH,
        )

    def total_start(step, carry):
        total_copy(step).start()
        return carry

    def total_wait(step, carry):
        total_copy(step).wait_recv()
        return carry

    def total_sent(step, carry):
        total_copy(step).wait_send()
        return carry

    lax.fori_loop(1, count, total_start, 0)
    lax.fori_loop(1, count, total_wait, 0)
    total_out[0, 0] = jnp.sum(total_window[...])
    lax.fori_loop(1, count, total_sent, 0)


def solution(mesh):
    count = mesh.shape["slab"]

    def shards(coords, charges, radii, screens, tile_lists, tile_counts, slab_fill):
        tiles = charges.shape[0] // LANES
        width = tile_lists.shape[1]
        block = jax.ShapeDtypeStruct((tiles, LANES), jnp.float32)
        smem = pl.BlockSpec(memory_space=pltpu.SMEM)
        vmem = pl.BlockSpec(memory_space=pltpu.VMEM)
        born, energy, total = pl.pallas_call(
            functools.partial(kernel, count),
            out_shape=(block, block, jax.ShapeDtypeStruct((1, 1), jnp.float32)),
            in_specs=[smem] * 3 + [vmem] * 4,
            out_specs=(vmem, vmem, smem),
            scratch_shapes=[
                pltpu.VMEM((5, 5 * tiles, LANES), jnp.float32),
                pltpu.VMEM((5 * tiles, LANES), jnp.float32),
                pltpu.VMEM((count, LANES), jnp.float32),
                pltpu.VMEM((tiles, 4, LANES, LANES), jnp.float32),
                pltpu.VMEM((tiles, 2, LANES, LANES), jnp.float32),
                pltpu.VMEM((width, 6, ROWS, LANES), jnp.float32),
                pltpu.VMEM((tiles, 3, LANES, LANES), jnp.float32),
                pltpu.VMEM((tiles, LANES), jnp.float32),
                pltpu.SemaphoreType.DMA((len(SHIFTS),)),
                pltpu.SemaphoreType.DMA((len(SHIFTS),)),
                pltpu.SemaphoreType.DMA((len(SHIFTS),)),
                pltpu.SemaphoreType.DMA((len(SHIFTS),)),
                pltpu.SemaphoreType.DMA((count,)),
                pltpu.SemaphoreType.DMA((count,)),
            ],
            compiler_params=pltpu.CompilerParams(
                collective_id=0, has_side_effects=True, vmem_limit_bytes=40 * 1024 * 1024
            ),
        )(
            tile_lists,
            tile_counts,
            slab_fill,
            coords,
            charges.reshape(tiles, LANES),
            radii.reshape(tiles, LANES),
            screens.reshape(tiles, LANES),
        )
        return born.reshape(-1), energy.reshape(-1), total.reshape(())

    placed = (
        P(None, "slab"),
        P("slab"),
        P("slab"),
        P("slab"),
        P("slab", None),
        P("slab"),
        P("slab"),
    )
    return jax.shard_map(
        shards, mesh=mesh, in_specs=placed, out_specs=(P("slab"), P("slab"), P()), check_vma=False
    )
```

```python
import functools

import jax
import jax.numpy as jnp
from jax import lax
from jax.experimental import pallas as pl
from jax.experimental.pallas import tpu as pltpu
from jax.sharding import PartitionSpec as P

OFFSET = 0.09
SOFTEN = 1.0
LOG2E = 1.4426950408889634
MESH = pl.DeviceIdType.MESH
SHIFTS = (1, -1, 2, -2)
LANES = 128
ROWS = 8


def squared_distance(own, partner):
    dx = own[0] - partner[0]
    dy = own[1] - partner[1]
    dz = own[2] - partner[2]
    return dx * dx + dy * dy + dz * dz


def born_parts(squared, offset_own, scaled, diagonal=None):
    soft = squared + SOFTEN
    inverse = lax.rsqrt(soft)
    distance = soft * inverse
    upper = distance + scaled
    reach = distance - scaled
    inner = jnp.maximum(offset_own, scaled - distance)
    lower = jnp.minimum(jnp.maximum(inner, reach), upper)
    both = pl.reciprocal(upper * lower, approx=True)
    over_lower = upper * both
    over_upper = lower * both
    apart = over_lower - over_upper
    bend = distance - scaled * scaled * inverse
    first = apart * (4.0 - bend * (over_lower + over_upper))
    second = inverse * jnp.log(lower * over_upper)
    third = (inner - offset_own) * over_lower
    if diagonal is not None:
        first = jnp.where(diagonal, 0.0, first)
        second = jnp.where(diagonal, 0.0, second)
        third = jnp.where(diagonal, 0.0, third)
    return first, second, third


def energy_part(squared, own_over, partner_over, partner_charge):
    scaled = squared * (own_over * partner_over)
    return partner_charge * lax.rsqrt(scaled + jnp.exp2(scaled * (-0.25 * LOG2E)))


def kernel(
    count,
    lists_in,
    counts_in,
    fill_in,
    coords_in,
    charges_in,
    radii_in,
    screens_in,
    born_out,
    energy_out,
    total_out,
    lists,
    counts,
    fill,
    coords,
    charges,
    radii,
    screens,
    window,
    born_window,
    over_window,
    charge_window,
    total_window,
    columns,
    born_columns,
    partners,
    sums,
    distances,
    collected,
    load_sems,
    window_send,
    window_recv,
    born_send,
    born_recv,
    total_send,
    total_recv,
):
    me = lax.axis_index("slab")
    tiles = charges.shape[0]
    width = lists.shape[0]
    steps = LANES // ROWS

    loads = [
        pltpu.make_async_copy(source, target, load_sems.at[place])
        for place, (source, target) in enumerate(
            (
                (fill_in, fill),
                (radii_in, radii),
                (screens_in, screens),
                (charges_in, charges),
                (coords_in, coords),
                (lists_in, lists),
                (counts_in, counts),
            )
        )
    ]
    for load in loads:
        load.start()

    barrier = pltpu.get_barrier_semaphore()

    def greet(step, carry):
        pl.semaphore_signal(
            barrier, inc=1, device_id=(lax.rem(me + step, count),), device_id_type=MESH
        )
        return carry

    lax.fori_loop(1, count, greet, 0)
    for load in loads:
        load.wait()

    slots = lax.broadcasted_iota(jnp.int32, (tiles, LANES), 0) * LANES
    slots = slots + lax.broadcasted_iota(jnp.int32, (tiles, LANES), 1)
    live = slots < fill[0]
    offset_own = jnp.where(live, radii[...] - OFFSET, 1.5 - OFFSET)
    home = pl.ds(2 * tiles, tiles)
    for component in range(3):
        for tile in range(tiles):
            window[component, 2 * tiles + tile : 2 * tiles + tile + 1, :] = coords[
                component : component + 1, tile * LANES : (tile + 1) * LANES
            ]
    window[3, home, :] = jnp.where(live, charges[...], 0.0)
    window[4, home, :] = jnp.where(live, screens[...] * (radii[...] - OFFSET), 0.0)

    def there(shift):
        return jnp.logical_and(me + shift >= 0, me + shift < count)

    def send(buffer, sems_out, sems_in, place, shift):
        def view(spot):
            rows = pl.ds(spot * tiles, tiles)
            return buffer.at[:, rows, :] if len(buffer.shape) == 3 else buffer.at[rows, :]

        return pltpu.make_async_remote_copy(
            src_ref=view(2),
            dst_ref=view(2 - shift),
            send_sem=sems_out.at[place],
            recv_sem=sems_in.at[place],
            device_id=(me + shift,),
            device_id_type=MESH,
        )

    def send_all(buffer, sems_out, sems_in):
        for place, shift in enumerate(SHIFTS):
            copy = send(buffer, sems_out, sems_in, place, shift)
            pl.when(there(shift))(copy.start)

    def wait_all(buffer, sems_out, sems_in):
        for place, shift in enumerate(SHIFTS):
            copy = send(buffer, sems_out, sems_in, place, shift)
            pl.when(there(shift))(copy.wait_send)
            pl.when(there(-shift))(copy.wait_recv)

    for shift in SHIFTS:

        @pl.when(jnp.logical_not(there(-shift)))
        def _():
            rows = pl.ds((2 - shift) * tiles, tiles)
            window[:, rows, :] = jnp.zeros((5, tiles, LANES), jnp.float32)
            born_window[rows, :] = jnp.ones((tiles, LANES), jnp.float32)

    pl.semaphore_wait(barrier, count - 1)
    send_all(window, window_send, window_recv)

    def diagonal_of(row):
        own_slot = lax.broadcasted_iota(jnp.int32, (ROWS, LANES), 0) + row
        return own_slot == lax.broadcasted_iota(jnp.int32, (ROWS, LANES), 1)

    def row_of(buffer, index):
        return jnp.broadcast_to(buffer[pl.ds(index, 1), :], (ROWS, LANES))

    def spread_columns(values, block, place):
        turned = values.T
        for tile in range(tiles):
            block[tile, place] = jnp.broadcast_to(turned[:, tile : tile + 1], (LANES, LANES))

    for component in range(3):
        spread_columns(window[component, home, :], columns, component)
    spread_columns(offset_own, columns, 3)
    collected[...] = jnp.zeros((LANES, LANES), jnp.float32)

    def collect(tile, rows, values):
        lane = lax.broadcasted_iota(jnp.int32, (ROWS, LANES), 1)
        row_sums = jnp.sum(values, axis=1, keepdims=True)
        collected[rows, :] = jnp.where(lane == tile, row_sums, collected[rows, :])

    def collected_rows():
        return collected[...].T[:tiles, :]

    def born_near(tile, carry):
        partner = [row_of(window.at[c], 2 * tiles + tile) for c in (0, 1, 2, 4)]
        for step in range(steps):
            rows = pl.ds(step * ROWS, ROWS)
            own = [columns[tile, c, rows, :] for c in range(4)]
            squared = squared_distance(own, partner)
            distances[tile, 0, rows, :] = squared
            terms = born_parts(squared, own[3], partner[3], diagonal_of(step * ROWS))
            for place, term in enumerate(terms):
                sums[tile, place, rows, :] = term
        return carry

    lax.fori_loop(0, tiles, born_near, 0)
    wait_all(window, window_send, window_recv)

    def born_far(tile, carry):
        for entry in range(1, width):
            index = lists[entry, tile]
            for place in range(3):
                partners[entry, place] = row_of(window.at[place], index)
            partners[entry, 3] = jnp.where(entry < counts[tile], row_of(window.at[4], index), 0.0)

        def one_step(step, inner):
            rows = pl.ds(pl.multiple_of(step * ROWS, ROWS), ROWS)
            own = [columns[tile, c, rows, :] for c in range(4)]
            totals = [sums[tile, c, rows, :] for c in range(3)]
            for entry in range(1, width):
                partner = [partners[entry, c] for c in range(4)]
                squared = squared_distance(own, partner)
                distances[tile, entry, rows, :] = squared
                terms = born_parts(squared, own[3], partner[3])
                totals = [old + term for old, term in zip(totals, terms)]
            collect(
                tile, rows, 0.125 * totals[0] + 0.25 * totals[1] + (2.0 / own[3]) * totals[2]
            )
            return inner

        lax.fori_loop(0, steps, one_step, 0, unroll=2)
        return carry

    lax.fori_loop(0, tiles, born_far, 0)

    radius_own = jnp.where(live, radii[...], 1.5)
    psi = collected_rows() * offset_own
    bending = jnp.tanh(psi - 0.8 * psi * psi + 4.85 * psi * psi * psi)
    born = 1.0 / (1.0 / offset_own - bending / radius_own)
    born_out[...] = jnp.where(live, born, 0.0)
    born_window[home, :] = jnp.where(live, born, 1.0)
    send_all(born_window, born_send, born_recv)

    own_over = 1.0 / born_window[home, :]
    over_window[home, :] = own_over
    charge_window[home, :] = window[3, home, :] * lax.rsqrt(born_window[home, :])
    spread_columns(own_over, born_columns, 0)

    def energy_near(tile, carry):
        partner = [row_of(buffer, 2 * tiles + tile) for buffer in (over_window, charge_window)]
        for step in range(steps):
            rows = pl.ds(step * ROWS, ROWS)
            sums[tile, 0, rows, :] = energy_part(
                distances[tile, 0, rows, :], born_columns[tile, 0, rows, :], *partner
            )
        return carry

    lax.fori_loop(0, tiles, energy_near, 0)
    wait_all(born_window, born_send, born_recv)
    over_window[...] = 1.0 / born_window[...]
    charge_window[...] = window[3] * lax.rsqrt(born_window[...])

    def energy_far(tile, carry):
        for entry in range(1, width):
            index = lists[entry, tile]
            partners[entry, 0] = row_of(over_window, index)
            partners[entry, 1] = jnp.where(
                entry < counts[tile], row_of(charge_window, index), 0.0
            )

        def one_step(step, inner):
            rows = pl.ds(pl.multiple_of(step * ROWS, ROWS), ROWS)
            own_column = born_columns[tile, 0, rows, :]
            total = sums[tile, 0, rows, :]
            for entry in range(1, width):
                total = total + energy_part(
                    distances[tile, entry, rows, :], own_column, partners[entry, 0], partners[entry, 1]
                )
            collect(tile, rows, total)
            return inner

        lax.fori_loop(0, steps, one_step, 0, unroll=2)
        return carry

    lax.fori_loop(0, tiles, energy_far, 0)

    energy = -0.5 * charge_window[home, :] * collected_rows()
    energy_out[...] = energy
    total_window[pl.ds(me, 1), :] = jnp.sum(energy, axis=0, keepdims=True)

    def total_copy(step):
        mine = total_window.at[pl.ds(me, 1), :]
        return pltpu.make_async_remote_copy(
            src_ref=mine,
            dst_ref=mine,
            send_sem=total_send.at[step],
            recv_sem=total_recv.at[step],
            device_id=(lax.rem(me + step, count),),
            device_id_type=MESH,
        )

    def total_start(step, carry):
        total_copy(step).start()
        return carry

    def total_wait(step, carry):
        total_copy(step).wait_recv()
        return carry

    def total_sent(step, carry):
        total_copy(step).wait_send()
        return carry

    lax.fori_loop(1, count, total_start, 0)
    lax.fori_loop(1, count, total_wait, 0)
    total_out[0, 0] = jnp.sum(total_window[...])
    lax.fori_loop(1, count, total_sent, 0)


def solution(mesh):
    count = mesh.shape["slab"]

    def shards(coords, charges, radii, screens, tile_lists, tile_counts, slab_fill):
        tiles = charges.shape[0] // LANES
        width = tile_lists.shape[1]
        block = jax.ShapeDtypeStruct((tiles, LANES), jnp.float32)
        smem = pl.BlockSpec(memory_space=pltpu.SMEM)
        hbm = pl.BlockSpec(memory_space=pltpu.HBM)
        vmem = pl.BlockSpec(memory_space=pltpu.VMEM)
        born, energy, total = pl.pallas_call(
            functools.partial(kernel, count),
            out_shape=(block, block, jax.ShapeDtypeStruct((1, 1), jnp.float32)),
            in_specs=[hbm] * 7,
            out_specs=(vmem, vmem, smem),
            scratch_shapes=[
                pltpu.SMEM((width, tiles), jnp.int32),
                pltpu.SMEM((tiles,), jnp.int32),
                pltpu.SMEM((1,), jnp.int32),
                pltpu.VMEM(coords.shape, jnp.float32),
                pltpu.VMEM((tiles, LANES), jnp.float32),
                pltpu.VMEM((tiles, LANES), jnp.float32),
                pltpu.VMEM((tiles, LANES), jnp.float32),
                pltpu.VMEM((5, 5 * tiles, LANES), jnp.float32),
                pltpu.VMEM((5 * tiles, LANES), jnp.float32),
                pltpu.VMEM((5 * tiles, LANES), jnp.float32),
                pltpu.VMEM((5 * tiles, LANES), jnp.float32),
                pltpu.VMEM((count, LANES), jnp.float32),
                pltpu.VMEM((tiles, 4, LANES, LANES), jnp.float32),
                pltpu.VMEM((tiles, 1, LANES, LANES), jnp.float32),
                pltpu.VMEM((width, 4, ROWS, LANES), jnp.float32),
                pltpu.VMEM((tiles, 3, LANES, LANES), jnp.float32),
                pltpu.VMEM((tiles, width, LANES, LANES), jnp.float32),
                pltpu.VMEM((LANES, LANES), jnp.float32),
                pltpu.SemaphoreType.DMA((7,)),
                pltpu.SemaphoreType.DMA((len(SHIFTS),)),
                pltpu.SemaphoreType.DMA((len(SHIFTS),)),
                pltpu.SemaphoreType.DMA((len(SHIFTS),)),
                pltpu.SemaphoreType.DMA((len(SHIFTS),)),
                pltpu.SemaphoreType.DMA((count,)),
                pltpu.SemaphoreType.DMA((count,)),
            ],
            compiler_params=pltpu.CompilerParams(
                collective_id=0, has_side_effects=True, vmem_limit_bytes=63463424

            ),
        )(
            tile_lists.T,
            tile_counts,
            slab_fill,
            coords,
            charges.reshape(tiles, LANES),
            radii.reshape(tiles, LANES),
            screens.reshape(tiles, LANES),
        )
        return born.reshape(-1), energy.reshape(-1), total.reshape(())

    placed = (
        P(None, "slab"),
        P("slab"),
        P("slab"),
        P("slab"),
        P("slab", None),
        P("slab"),
        P("slab"),
    )
    return jax.shard_map(
        shards, mesh=mesh, in_specs=placed, out_specs=(P("slab"), P("slab"), P()), check_vma=False
    )
```

```python
import functools

import jax
import jax.numpy as jnp
from jax import lax
from jax.experimental import pallas as pl
from jax.experimental.pallas import tpu as pltpu
from jax.sharding import PartitionSpec as P

OFFSET = 0.09
SOFTEN = 1.0
LOG2E = 1.4426950408889634
MESH = pl.DeviceIdType.MESH
SHIFTS = (1, -1, 2, -2)
LANES = 128
ROWS = 8


def squared_distance(own, partner):
    dx = own[0] - partner[0]
    dy = own[1] - partner[1]
    dz = own[2] - partner[2]
    return dx * dx + dy * dy + dz * dz


def born_parts(squared, offset_own, scaled, diagonal=None):
    soft = squared + SOFTEN
    inverse = lax.rsqrt(soft)
    distance = soft * inverse
    upper = distance + scaled
    reach = distance - scaled
    inner = jnp.maximum(offset_own, scaled - distance)
    lower = jnp.minimum(jnp.maximum(inner, reach), upper)
    both = pl.reciprocal(upper * lower, approx=True)
    over_lower = upper * both
    over_upper = lower * both
    apart = over_lower - over_upper
    bend = distance - scaled * scaled * inverse
    first = apart * (4.0 - bend * (over_lower + over_upper))
    second = inverse * jnp.log(lower * over_upper)
    third = (inner - offset_own) * over_lower
    if diagonal is not None:
        first = jnp.where(diagonal, 0.0, first)
        second = jnp.where(diagonal, 0.0, second)
        third = jnp.where(diagonal, 0.0, third)
    return first, second, third


def energy_part(squared, own_over, partner_over, partner_charge):
    scaled = squared * (own_over * partner_over)
    return partner_charge * lax.rsqrt(scaled + jnp.exp2(scaled * (-0.25 * LOG2E)))


def kernel(
    count,
    lists_in,
    counts_in,
    fill_in,
    coords_in,
    charges_in,
    radii_in,
    screens_in,
    born_out,
    energy_out,
    total_out,
    lists,
    counts,
    fill,
    coords,
    charges,
    radii,
    screens,
    window,
    born_window,
    over_window,
    charge_window,
    total_window,
    columns,
    born_columns,
    partners,
    sums,
    distances,
    result,
    load_sems,
    window_send,
    window_recv,
    born_send,
    born_recv,
    total_send,
    total_recv,
):
    me = lax.axis_index("slab")
    tiles = charges.shape[0]
    width = lists.shape[0]
    steps = LANES // ROWS

    loads = [
        pltpu.make_async_copy(source, target, load_sems.at[place])
        for place, (source, target) in enumerate(
            (
                (fill_in, fill),
                (radii_in, radii),
                (screens_in, screens),
                (charges_in, charges),
                (coords_in, coords),
                (lists_in, lists),
                (counts_in, counts),
            )
        )
    ]
    for load in loads:
        load.start()

    barrier = pltpu.get_barrier_semaphore()

    def greet(step, carry):
        pl.semaphore_signal(
            barrier, inc=1, device_id=(lax.rem(me + step, count),), device_id_type=MESH
        )
        return carry

    lax.fori_loop(1, count, greet, 0)
    for load in loads:
        load.wait()

    slots = lax.broadcasted_iota(jnp.int32, (tiles, LANES), 0) * LANES
    slots = slots + lax.broadcasted_iota(jnp.int32, (tiles, LANES), 1)
    live = slots < fill[0]
    offset_own = jnp.where(live, radii[...] - OFFSET, 1.5 - OFFSET)
    home = pl.ds(2 * tiles, tiles)
    for component in range(3):
        for tile in range(tiles):
            window[component, 2 * tiles + tile : 2 * tiles + tile + 1, :] = coords[
                component : component + 1, tile * LANES : (tile + 1) * LANES
            ]
    window[3, home, :] = jnp.where(live, charges[...], 0.0)
    window[4, home, :] = jnp.where(live, screens[...] * (radii[...] - OFFSET), 0.0)

    def there(shift):
        return jnp.logical_and(me + shift >= 0, me + shift < count)

    def send(buffer, sems_out, sems_in, place, shift):
        def view(spot):
            rows = pl.ds(spot * tiles, tiles)
            return buffer.at[:, rows, :] if len(buffer.shape) == 3 else buffer.at[rows, :]

        return pltpu.make_async_remote_copy(
            src_ref=view(2),
            dst_ref=view(2 - shift),
            send_sem=sems_out.at[place],
            recv_sem=sems_in.at[place],
            device_id=(me + shift,),
            device_id_type=MESH,
        )

    def send_all(buffer, sems_out, sems_in):
        for place, shift in enumerate(SHIFTS):
            copy = send(buffer, sems_out, sems_in, place, shift)
            pl.when(there(shift))(copy.start)

    def wait_all(buffer, sems_out, sems_in):
        for place, shift in enumerate(SHIFTS):
            copy = send(buffer, sems_out, sems_in, place, shift)
            pl.when(there(shift))(copy.wait_send)
            pl.when(there(-shift))(copy.wait_recv)

    for shift in SHIFTS:

        @pl.when(jnp.logical_not(there(-shift)))
        def _():
            rows = pl.ds((2 - shift) * tiles, tiles)
            window[:, rows, :] = jnp.zeros((5, tiles, LANES), jnp.float32)
            born_window[rows, :] = jnp.ones((tiles, LANES), jnp.float32)

    pl.semaphore_wait(barrier, count - 1)
    send_all(window, window_send, window_recv)

    def diagonal_of(row):
        own_slot = lax.broadcasted_iota(jnp.int32, (ROWS, LANES), 0) + row
        return own_slot == lax.broadcasted_iota(jnp.int32, (ROWS, LANES), 1)

    def row_of(buffer, index):
        return jnp.broadcast_to(buffer[pl.ds(index, 1), :], (ROWS, LANES))

    def spread_columns(values, block, place):
        turned = values.T
        for tile in range(tiles):
            block[tile, place] = jnp.broadcast_to(turned[:, tile : tile + 1], (LANES, LANES))

    for component in range(3):
        spread_columns(window[component, home, :], columns, component)
    spread_columns(offset_own, columns, 3)

    ones = jnp.ones((ROWS, LANES), jnp.float32)

    def row_sums():
        for tile in range(tiles):
            added = lax.dot_general(
                ones,
                sums[tile, 0],
                (((1,), (1,)), ((), ())),
                precision=lax.Precision.HIGHEST,
                preferred_element_type=jnp.float32,
            )
            result[tile : tile + 1, :] = added[:1]
        return result[...]

    def born_near(tile, carry):
        partner = [row_of(window.at[c], 2 * tiles + tile) for c in (0, 1, 2, 4)]
        for step in range(steps):
            rows = pl.ds(step * ROWS, ROWS)
            own = [columns[tile, c, rows, :] for c in range(4)]
            squared = squared_distance(own, partner)
            distances[tile, 0, rows, :] = squared
            terms = born_parts(squared, own[3], partner[3], diagonal_of(step * ROWS))
            for place, term in enumerate(terms):
                sums[tile, place, rows, :] = term
        return carry

    lax.fori_loop(0, tiles, born_near, 0)
    wait_all(window, window_send, window_recv)

    def born_far(tile, carry):
        for entry in range(1, width):
            index = lists[entry, tile]
            for place in range(3):
                partners[entry, place] = row_of(window.at[place], index)
            partners[entry, 3] = jnp.where(entry < counts[tile], row_of(window.at[4], index), 0.0)

        def one_step(step, inner):
            rows = pl.ds(pl.multiple_of(step * ROWS, ROWS), ROWS)
            own = [columns[tile, c, rows, :] for c in range(4)]
            totals = [sums[tile, c, rows, :] for c in range(3)]
            for entry in range(1, width):
                partner = [partners[entry, c] for c in range(4)]
                squared = squared_distance(own, partner)
                distances[tile, entry, rows, :] = squared
                terms = born_parts(squared, own[3], partner[3])
                totals = [old + term for old, term in zip(totals, terms)]
            sums[tile, 0, rows, :] = (
                0.125 * totals[0] + 0.25 * totals[1] + (2.0 / own[3]) * totals[2]
            )
            return inner

        lax.fori_loop(0, steps, one_step, 0, unroll=4)
        return carry

    lax.fori_loop(0, tiles, born_far, 0)

    radius_own = jnp.where(live, radii[...], 1.5)
    psi = row_sums() * offset_own
    bending = jnp.tanh(psi - 0.8 * psi * psi + 4.85 * psi * psi * psi)
    born = 1.0 / (1.0 / offset_own - bending / radius_own)
    born_out[...] = jnp.where(live, born, 0.0)
    born_window[home, :] = jnp.where(live, born, 1.0)
    send_all(born_window, born_send, born_recv)

    own_over = 1.0 / born_window[home, :]
    over_window[home, :] = own_over
    charge_window[home, :] = window[3, home, :] * lax.rsqrt(born_window[home, :])
    spread_columns(own_over, born_columns, 0)

    def energy_near(tile, carry):
        partner = [row_of(buffer, 2 * tiles + tile) for buffer in (over_window, charge_window)]
        for step in range(steps):
            rows = pl.ds(step * ROWS, ROWS)
            sums[tile, 0, rows, :] = energy_part(
                distances[tile, 0, rows, :], born_columns[tile, 0, rows, :], *partner
            )
        return carry

    lax.fori_loop(0, tiles, energy_near, 0)
    wait_all(born_window, born_send, born_recv)
    over_window[...] = 1.0 / born_window[...]
    charge_window[...] = window[3] * lax.rsqrt(born_window[...])

    def energy_far(tile, carry):
        for entry in range(1, width):
            index = lists[entry, tile]
            partners[entry, 0] = row_of(over_window, index)
            partners[entry, 1] = jnp.where(
                entry < counts[tile], row_of(charge_window, index), 0.0
            )

        def one_step(step, inner):
            rows = pl.ds(pl.multiple_of(step * ROWS, ROWS), ROWS)
            own_column = born_columns[tile, 0, rows, :]
            total = sums[tile, 0, rows, :]
            for entry in range(1, width):
                total = total + energy_part(
                    distances[tile, entry, rows, :], own_column, partners[entry, 0], partners[entry, 1]
                )
            sums[tile, 0, rows, :] = total
            return inner

        lax.fori_loop(0, steps, one_step, 0, unroll=4)
        return carry

    lax.fori_loop(0, tiles, energy_far, 0)

    energy = -0.5 * charge_window[home, :] * row_sums()
    energy_out[...] = energy
    total_window[pl.ds(me, 1), :] = jnp.sum(energy, axis=0, keepdims=True)

    def total_copy(step):
        mine = total_window.at[pl.ds(me, 1), :]
        return pltpu.make_async_remote_copy(
            src_ref=mine,
            dst_ref=mine,
            send_sem=total_send.at[step],
            recv_sem=total_recv.at[step],
            device_id=(lax.rem(me + step, count),),
            device_id_type=MESH,
        )

    def total_start(step, carry):
        total_copy(step).start()
        return carry

    def total_wait(step, carry):
        total_copy(step).wait_recv()
        return carry

    def total_sent(step, carry):
        total_copy(step).wait_send()
        return carry

    lax.fori_loop(1, count, total_start, 0)
    lax.fori_loop(1, count, total_wait, 0)
    total_out[0, 0] = jnp.sum(total_window[...])
    lax.fori_loop(1, count, total_sent, 0)


def hand_over(born, energy, born_out, energy_out):
    born_out[...] = born[...]
    energy_out[...] = energy[...]


def solution(mesh):
    count = mesh.shape["slab"]

    def shards(coords, charges, radii, screens, tile_lists, tile_counts, slab_fill):
        tiles = charges.shape[0] // LANES
        width = tile_lists.shape[1]
        block = jax.ShapeDtypeStruct((tiles, LANES), jnp.float32)
        smem = pl.BlockSpec(memory_space=pltpu.SMEM)
        hbm = pl.BlockSpec(memory_space=pltpu.HBM)
        vmem = pl.BlockSpec(memory_space=pltpu.VMEM)
        born, energy, total = pl.pallas_call(
            functools.partial(kernel, count),
            out_shape=(block, block, jax.ShapeDtypeStruct((1, 1), jnp.float32)),
            in_specs=[hbm] * 7,
            out_specs=(vmem, vmem, smem),
            scratch_shapes=[
                pltpu.SMEM((width, tiles), jnp.int32),
                pltpu.SMEM((tiles,), jnp.int32),
                pltpu.SMEM((1,), jnp.int32),
                pltpu.VMEM(coords.shape, jnp.float32),
                pltpu.VMEM((tiles, LANES), jnp.float32),
                pltpu.VMEM((tiles, LANES), jnp.float32),
                pltpu.VMEM((tiles, LANES), jnp.float32),
                pltpu.VMEM((5, 5 * tiles, LANES), jnp.float32),
                pltpu.VMEM((5 * tiles, LANES), jnp.float32),
                pltpu.VMEM((5 * tiles, LANES), jnp.float32),
                pltpu.VMEM((5 * tiles, LANES), jnp.float32),
                pltpu.VMEM((count, LANES), jnp.float32),
                pltpu.VMEM((tiles, 4, LANES, LANES), jnp.float32),
                pltpu.VMEM((tiles, 1, LANES, LANES), jnp.float32),
                pltpu.VMEM((width, 4, ROWS, LANES), jnp.float32),
                pltpu.VMEM((tiles, 3, LANES, LANES), jnp.float32),
                pltpu.VMEM((tiles, width, LANES, LANES), jnp.float32),
                pltpu.VMEM((tiles, LANES), jnp.float32),
                pltpu.SemaphoreType.DMA((7,)),
                pltpu.SemaphoreType.DMA((len(SHIFTS),)),
                pltpu.SemaphoreType.DMA((len(SHIFTS),)),
                pltpu.SemaphoreType.DMA((len(SHIFTS),)),
                pltpu.SemaphoreType.DMA((len(SHIFTS),)),
                pltpu.SemaphoreType.DMA((count,)),
                pltpu.SemaphoreType.DMA((count,)),
            ],
            compiler_params=pltpu.CompilerParams(
                collective_id=0, has_side_effects=True, vmem_limit_bytes=63463424

            ),
        )(
            tile_lists.T,
            tile_counts,
            slab_fill,
            coords,
            charges.reshape(tiles, LANES),
            radii.reshape(tiles, LANES),
            screens.reshape(tiles, LANES),
        )
        born, energy = pl.pallas_call(
            hand_over, out_shape=(block, block), in_specs=[vmem] * 2, out_specs=(vmem, vmem)
        )(born, energy)
        return born.reshape(-1), energy.reshape(-1), total.reshape(())

    placed = (
        P(None, "slab"),
        P("slab"),
        P("slab"),
        P("slab"),
        P("slab", None),
        P("slab"),
        P("slab"),
    )
    return jax.shard_map(
        shards, mesh=mesh, in_specs=placed, out_specs=(P("slab"), P("slab"), P()), check_vma=False
    )
```

```python
import functools

import jax
import jax.numpy as jnp
from jax import lax
from jax.experimental import pallas as pl
from jax.experimental.pallas import tpu as pltpu
from jax.sharding import PartitionSpec as P

OFFSET = 0.09
SOFTEN = 1.0
LOG2E = 1.4426950408889634
MESH = pl.DeviceIdType.MESH
SHIFTS = (1, -1, 2, -2)
LANES = 128
ROWS = 8


def squared_distance(own, partner):
    dx = own[0] - partner[0]
    dy = own[1] - partner[1]
    dz = own[2] - partner[2]
    return dx * dx + dy * dy + dz * dz


def born_parts(squared, offset_own, scaled, diagonal=None):
    soft = squared + SOFTEN
    inverse = lax.rsqrt(soft)
    distance = soft * inverse
    upper = distance + scaled
    reach = distance - scaled
    inner = jnp.maximum(offset_own, scaled - distance)
    lower = jnp.minimum(jnp.maximum(inner, reach), upper)
    both = pl.reciprocal(upper * lower, approx=True)
    over_lower = upper * both
    over_upper = lower * both
    apart = over_lower - over_upper
    bend = distance - scaled * scaled * inverse
    first = apart * (4.0 - bend * (over_lower + over_upper))
    second = inverse * jnp.log(lower * over_upper)
    third = (inner - offset_own) * over_lower
    if diagonal is not None:
        first = jnp.where(diagonal, 0.0, first)
        second = jnp.where(diagonal, 0.0, second)
        third = jnp.where(diagonal, 0.0, third)
    return first, second, third


def energy_part(squared, own_over, partner_over, partner_charge):
    scaled = squared * (own_over * partner_over)
    return partner_charge * lax.rsqrt(scaled + jnp.exp2(scaled * (-0.25 * LOG2E)))


def kernel(
    count,
    lists_in,
    counts_in,
    fill_in,
    coords_in,
    charges_in,
    radii_in,
    screens_in,
    born_out,
    energy_out,
    total_out,
    lists,
    counts,
    fill,
    coords,
    charges,
    radii,
    screens,
    window,
    born_window,
    over_window,
    charge_window,
    total_window,
    columns,
    born_columns,
    partners,
    sums,
    distances,
    load_sems,
    window_send,
    window_recv,
    born_send,
    born_recv,
    total_send,
    total_recv,
):
    me = lax.axis_index("slab")
    tiles = charges.shape[0]
    width = lists.shape[0]
    steps = LANES // ROWS

    loads = [
        pltpu.make_async_copy(source, target, load_sems.at[place])
        for place, (source, target) in enumerate(
            (
                (fill_in, fill),
                (radii_in, radii),
                (screens_in, screens),
                (charges_in, charges),
                (coords_in, coords),
                (lists_in, lists),
                (counts_in, counts),
            )
        )
    ]
    for load in loads:
        load.start()

    barrier = pltpu.get_barrier_semaphore()

    def greet(step, carry):
        pl.semaphore_signal(
            barrier, inc=1, device_id=(lax.rem(me + step, count),), device_id_type=MESH
        )
        return carry

    lax.fori_loop(1, count, greet, 0)
    for load in loads:
        load.wait()

    slots = lax.broadcasted_iota(jnp.int32, (tiles, LANES), 0) * LANES
    slots = slots + lax.broadcasted_iota(jnp.int32, (tiles, LANES), 1)
    live = slots < fill[0]
    offset_own = jnp.where(live, radii[...] - OFFSET, 1.5 - OFFSET)
    home = pl.ds(2 * tiles, tiles)
    for component in range(3):
        for tile in range(tiles):
            window[component, 2 * tiles + tile : 2 * tiles + tile + 1, :] = coords[
                component : component + 1, tile * LANES : (tile + 1) * LANES
            ]
    window[3, home, :] = jnp.where(live, charges[...], 0.0)
    window[4, home, :] = jnp.where(live, screens[...] * (radii[...] - OFFSET), 0.0)

    def there(shift):
        return jnp.logical_and(me + shift >= 0, me + shift < count)

    def send(buffer, sems_out, sems_in, place, shift):
        def view(spot):
            rows = pl.ds(spot * tiles, tiles)
            return buffer.at[:, rows, :] if len(buffer.shape) == 3 else buffer.at[rows, :]

        return pltpu.make_async_remote_copy(
            src_ref=view(2),
            dst_ref=view(2 - shift),
            send_sem=sems_out.at[place],
            recv_sem=sems_in.at[place],
            device_id=(me + shift,),
            device_id_type=MESH,
        )

    def send_all(buffer, sems_out, sems_in):
        for place, shift in enumerate(SHIFTS):
            copy = send(buffer, sems_out, sems_in, place, shift)
            pl.when(there(shift))(copy.start)

    def wait_all(buffer, sems_out, sems_in):
        for place, shift in enumerate(SHIFTS):
            copy = send(buffer, sems_out, sems_in, place, shift)
            pl.when(there(shift))(copy.wait_send)
            pl.when(there(-shift))(copy.wait_recv)

    for shift in SHIFTS:

        @pl.when(jnp.logical_not(there(-shift)))
        def _():
            rows = pl.ds((2 - shift) * tiles, tiles)
            window[:, rows, :] = jnp.zeros((5, tiles, LANES), jnp.float32)
            born_window[rows, :] = jnp.ones((tiles, LANES), jnp.float32)

    pl.semaphore_wait(barrier, count - 1)
    send_all(window, window_send, window_recv)

    def diagonal_of(row):
        own_slot = lax.broadcasted_iota(jnp.int32, (ROWS, LANES), 0) + row
        return own_slot == lax.broadcasted_iota(jnp.int32, (ROWS, LANES), 1)

    def row_of(buffer, index):
        return jnp.broadcast_to(buffer[pl.ds(index, 1), :], (ROWS, LANES))

    def spread_columns(values, block, place):
        turned = values.T
        for tile in range(tiles):
            block[tile, place] = jnp.broadcast_to(turned[:, tile : tile + 1], (LANES, LANES))

    for component in range(3):
        spread_columns(window[component, home, :], columns, component)
    spread_columns(offset_own, columns, 3)

    lane = lax.broadcasted_iota(jnp.int32, (LANES, LANES), 1)

    def row_sums():
        gathered = jnp.zeros((LANES, LANES), jnp.float32)
        for tile in range(tiles):
            added = jnp.sum(sums[tile, 0], axis=1, keepdims=True)
            gathered = jnp.where(lane == tile, added, gathered)
        return gathered.T[:tiles, :]

    def born_near(tile, carry):
        partner = [row_of(window.at[c], 2 * tiles + tile) for c in (0, 1, 2, 4)]
        for step in range(steps):
            rows = pl.ds(step * ROWS, ROWS)
            own = [columns[tile, c, rows, :] for c in range(4)]
            squared = squared_distance(own, partner)
            distances[tile, 0, rows, :] = squared
            terms = born_parts(squared, own[3], partner[3], diagonal_of(step * ROWS))
            for place, term in enumerate(terms):
                sums[tile, place, rows, :] = term
        return carry

    lax.fori_loop(0, tiles, born_near, 0)
    wait_all(window, window_send, window_recv)

    def born_far(tile, carry):
        for entry in range(1, width):
            index = lists[entry, tile]
            for place in range(3):
                partners[entry, place] = row_of(window.at[place], index)
            partners[entry, 3] = jnp.where(entry < counts[tile], row_of(window.at[4], index), 0.0)

        def one_step(step, inner):
            rows = pl.ds(pl.multiple_of(step * ROWS, ROWS), ROWS)
            own = [columns[tile, c, rows, :] for c in range(4)]
            totals = [sums[tile, c, rows, :] for c in range(3)]
            for entry in range(1, width):
                partner = [partners[entry, c] for c in range(4)]
                squared = squared_distance(own, partner)
                distances[tile, entry, rows, :] = squared
                terms = born_parts(squared, own[3], partner[3])
                totals = [old + term for old, term in zip(totals, terms)]
            sums[tile, 0, rows, :] = (
                0.125 * totals[0] + 0.25 * totals[1] + (2.0 / own[3]) * totals[2]
            )
            return inner

        lax.fori_loop(0, steps, one_step, 0, unroll=steps)
        return carry

    lax.fori_loop(0, tiles, born_far, 0)

    radius_own = jnp.where(live, radii[...], 1.5)
    psi = row_sums() * offset_own
    bending = jnp.tanh(psi - 0.8 * psi * psi + 4.85 * psi * psi * psi)
    born = 1.0 / (1.0 / offset_own - bending / radius_own)
    born_out[...] = jnp.where(live, born, 0.0)
    born_window[home, :] = jnp.where(live, born, 1.0)
    send_all(born_window, born_send, born_recv)

    own_over = 1.0 / born_window[home, :]
    over_window[home, :] = own_over
    charge_window[home, :] = window[3, home, :] * lax.rsqrt(born_window[home, :])
    spread_columns(own_over, born_columns, 0)

    def energy_near(tile, carry):
        partner = [row_of(buffer, 2 * tiles + tile) for buffer in (over_window, charge_window)]
        for step in range(steps):
            rows = pl.ds(step * ROWS, ROWS)
            sums[tile, 0, rows, :] = energy_part(
                distances[tile, 0, rows, :], born_columns[tile, 0, rows, :], *partner
            )
        return carry

    lax.fori_loop(0, tiles, energy_near, 0)
    wait_all(born_window, born_send, born_recv)
    over_window[...] = 1.0 / born_window[...]
    charge_window[...] = window[3] * lax.rsqrt(born_window[...])

    def energy_far(tile, carry):
        for entry in range(1, width):
            index = lists[entry, tile]
            partners[entry, 0] = row_of(over_window, index)
            partners[entry, 1] = jnp.where(
                entry < counts[tile], row_of(charge_window, index), 0.0
            )

        def one_step(step, inner):
            rows = pl.ds(pl.multiple_of(step * ROWS, ROWS), ROWS)
            own_column = born_columns[tile, 0, rows, :]
            total = sums[tile, 0, rows, :]
            for entry in range(1, width):
                total = total + energy_part(
                    distances[tile, entry, rows, :], own_column, partners[entry, 0], partners[entry, 1]
                )
            sums[tile, 0, rows, :] = total
            return inner

        lax.fori_loop(0, steps, one_step, 0, unroll=steps)
        return carry

    lax.fori_loop(0, tiles, energy_far, 0)

    energy = -0.5 * charge_window[home, :] * row_sums()
    energy_out[...] = energy
    total_window[pl.ds(me, 1), :] = jnp.sum(energy, axis=0, keepdims=True)

    def total_copy(step):
        mine = total_window.at[pl.ds(me, 1), :]
        return pltpu.make_async_remote_copy(
            src_ref=mine,
            dst_ref=mine,
            send_sem=total_send.at[step],
            recv_sem=total_recv.at[step],
            device_id=(lax.rem(me + step, count),),
            device_id_type=MESH,
        )

    def total_start(step, carry):
        total_copy(step).start()
        return carry

    def total_wait(step, carry):
        total_copy(step).wait_recv()
        return carry

    def total_sent(step, carry):
        total_copy(step).wait_send()
        return carry

    lax.fori_loop(1, count, total_start, 0)
    lax.fori_loop(1, count, total_wait, 0)
    total_out[0, 0] = jnp.sum(total_window[...])
    lax.fori_loop(1, count, total_sent, 0)


def hand_over(born, energy, born_out, energy_out):
    born_out[...] = born[...]
    energy_out[...] = energy[...]


def solution(mesh):
    count = mesh.shape["slab"]

    def shards(coords, charges, radii, screens, tile_lists, tile_counts, slab_fill):
        tiles = charges.shape[0] // LANES
        width = tile_lists.shape[1]
        block = jax.ShapeDtypeStruct((tiles, LANES), jnp.float32)
        smem = pl.BlockSpec(memory_space=pltpu.SMEM)
        hbm = pl.BlockSpec(memory_space=pltpu.HBM)
        vmem = pl.BlockSpec(memory_space=pltpu.VMEM)
        born, energy, total = pl.pallas_call(
            functools.partial(kernel, count),
            out_shape=(block, block, jax.ShapeDtypeStruct((1, 1), jnp.float32)),
            in_specs=[hbm] * 7,
            out_specs=(vmem, vmem, smem),
            scratch_shapes=[
                pltpu.SMEM((width, tiles), jnp.int32),
                pltpu.SMEM((tiles,), jnp.int32),
                pltpu.SMEM((1,), jnp.int32),
                pltpu.VMEM(coords.shape, jnp.float32),
                pltpu.VMEM((tiles, LANES), jnp.float32),
                pltpu.VMEM((tiles, LANES), jnp.float32),
                pltpu.VMEM((tiles, LANES), jnp.float32),
                pltpu.VMEM((5, 5 * tiles, LANES), jnp.float32),
                pltpu.VMEM((5 * tiles, LANES), jnp.float32),
                pltpu.VMEM((5 * tiles, LANES), jnp.float32),
                pltpu.VMEM((5 * tiles, LANES), jnp.float32),
                pltpu.VMEM((count, LANES), jnp.float32),
                pltpu.VMEM((tiles, 4, LANES, LANES), jnp.float32),
                pltpu.VMEM((tiles, 1, LANES, LANES), jnp.float32),
                pltpu.VMEM((width, 4, ROWS, LANES), jnp.float32),
                pltpu.VMEM((tiles, 3, LANES, LANES), jnp.float32),
                pltpu.VMEM((tiles, width, LANES, LANES), jnp.float32),
                pltpu.SemaphoreType.DMA((7,)),
                pltpu.SemaphoreType.DMA((len(SHIFTS),)),
                pltpu.SemaphoreType.DMA((len(SHIFTS),)),
                pltpu.SemaphoreType.DMA((len(SHIFTS),)),
                pltpu.SemaphoreType.DMA((len(SHIFTS),)),
                pltpu.SemaphoreType.DMA((count,)),
                pltpu.SemaphoreType.DMA((count,)),
            ],
            compiler_params=pltpu.CompilerParams(
                collective_id=0, has_side_effects=True, vmem_limit_bytes=63463424

            ),
        )(
            tile_lists.T,
            tile_counts,
            slab_fill,
            coords,
            charges.reshape(tiles, LANES),
            radii.reshape(tiles, LANES),
            screens.reshape(tiles, LANES),
        )
        born, energy = pl.pallas_call(
            hand_over, out_shape=(block, block), in_specs=[vmem] * 2, out_specs=(vmem, vmem)
        )(born, energy)
        return born.reshape(-1), energy.reshape(-1), total.reshape(())

    placed = (
        P(None, "slab"),
        P("slab"),
        P("slab"),
        P("slab"),
        P("slab", None),
        P("slab"),
        P("slab"),
    )
    return jax.shard_map(
        shards, mesh=mesh, in_specs=placed, out_specs=(P("slab"), P("slab"), P()), check_vma=False
    )
```

```python
import functools

import jax
import jax.numpy as jnp
from jax import lax
from jax.experimental import pallas as pl
from jax.experimental.pallas import tpu as pltpu
from jax.sharding import PartitionSpec as P

OFFSET = 0.09
SOFTEN = 1.0
LOG2E = 1.4426950408889634
MESH = pl.DeviceIdType.MESH
SHIFTS = (1, -1, 2, -2)
LANES = 128
ROWS = 8


def squared_distance(own, partner):
    dx = own[0] - partner[0]
    dy = own[1] - partner[1]
    dz = own[2] - partner[2]
    return dx * dx + dy * dy + dz * dz


def born_parts(squared, offset_own, scaled, scaled_square, diagonal=None):
    soft = squared + SOFTEN
    inverse = lax.rsqrt(soft)
    distance = soft * inverse
    upper = distance + scaled
    reach = distance - scaled
    inner = jnp.maximum(offset_own, scaled - distance)
    lower = jnp.minimum(jnp.maximum(inner, reach), upper)
    both = pl.reciprocal(upper * lower, approx=True)
    over_lower = upper * both
    over_upper = lower * both
    apart = over_lower - over_upper
    bend = distance - scaled_square * inverse
    first = apart * (4.0 - bend * (over_lower + over_upper))
    second = inverse * jnp.log(lower * over_upper)
    third = (inner - offset_own) * over_lower
    if diagonal is not None:
        first = jnp.where(diagonal, 0.0, first)
        second = jnp.where(diagonal, 0.0, second)
        third = jnp.where(diagonal, 0.0, third)
    return first, second, third


def energy_part(squared, own_over, partner_over, partner_charge):
    scaled = squared * (own_over * partner_over)
    return partner_charge * lax.rsqrt(scaled + jnp.exp2(scaled * (-0.25 * LOG2E)))


def kernel(
    count,
    lists_in,
    counts_in,
    fill_in,
    coords_in,
    charges_in,
    radii_in,
    screens_in,
    born_out,
    energy_out,
    total_out,
    lists,
    counts,
    fill,
    coords,
    charges,
    radii,
    screens,
    window,
    born_window,
    over_window,
    charge_window,
    total_window,
    columns,
    born_columns,
    partners,
    sums,
    distances,
    load_sems,
    window_send,
    window_recv,
    born_send,
    born_recv,
    total_send,
    total_recv,
):
    me = lax.axis_index("slab")
    tiles = charges.shape[0]
    width = lists.shape[0]
    steps = LANES // ROWS

    loads = [
        pltpu.make_async_copy(source, target, load_sems.at[place])
        for place, (source, target) in enumerate(
            (
                (fill_in, fill),
                (radii_in, radii),
                (screens_in, screens),
                (charges_in, charges),
                (coords_in, coords),
                (lists_in, lists),
                (counts_in, counts),
            )
        )
    ]
    for load in loads:
        load.start()

    barrier = pltpu.get_barrier_semaphore()

    def greet(step, carry):
        pl.semaphore_signal(
            barrier, inc=1, device_id=(lax.rem(me + step, count),), device_id_type=MESH
        )
        return carry

    lax.fori_loop(1, count, greet, 0)
    for load in loads:
        load.wait()

    slots = lax.broadcasted_iota(jnp.int32, (tiles, LANES), 0) * LANES
    slots = slots + lax.broadcasted_iota(jnp.int32, (tiles, LANES), 1)
    live = slots < fill[0]
    offset_own = jnp.where(live, radii[...] - OFFSET, 1.5 - OFFSET)
    home = pl.ds(2 * tiles, tiles)
    for component in range(3):
        for tile in range(tiles):
            window[component, 2 * tiles + tile : 2 * tiles + tile + 1, :] = coords[
                component : component + 1, tile * LANES : (tile + 1) * LANES
            ]
    window[3, home, :] = jnp.where(live, charges[...], 0.0)
    window[4, home, :] = jnp.where(live, screens[...] * (radii[...] - OFFSET), 0.0)

    def there(shift):
        return jnp.logical_and(me + shift >= 0, me + shift < count)

    def send(buffer, sems_out, sems_in, place, shift):
        def view(spot):
            rows = pl.ds(spot * tiles, tiles)
            return buffer.at[:, rows, :] if len(buffer.shape) == 3 else buffer.at[rows, :]

        return pltpu.make_async_remote_copy(
            src_ref=view(2),
            dst_ref=view(2 - shift),
            send_sem=sems_out.at[place],
            recv_sem=sems_in.at[place],
            device_id=(me + shift,),
            device_id_type=MESH,
        )

    def send_all(buffer, sems_out, sems_in):
        for place, shift in enumerate(SHIFTS):
            copy = send(buffer, sems_out, sems_in, place, shift)
            pl.when(there(shift))(copy.start)

    def wait_all(buffer, sems_out, sems_in):
        for place, shift in enumerate(SHIFTS):
            copy = send(buffer, sems_out, sems_in, place, shift)
            pl.when(there(shift))(copy.wait_send)
            pl.when(there(-shift))(copy.wait_recv)

    for shift in SHIFTS:

        @pl.when(jnp.logical_not(there(-shift)))
        def _():
            rows = pl.ds((2 - shift) * tiles, tiles)
            window[:, rows, :] = jnp.zeros((5, tiles, LANES), jnp.float32)
            born_window[rows, :] = jnp.ones((tiles, LANES), jnp.float32)

    pl.semaphore_wait(barrier, count - 1)
    send_all(window, window_send, window_recv)

    def diagonal_of(row):
        own_slot = lax.broadcasted_iota(jnp.int32, (ROWS, LANES), 0) + row
        return own_slot == lax.broadcasted_iota(jnp.int32, (ROWS, LANES), 1)

    def row_of(buffer, index):
        return jnp.broadcast_to(buffer[pl.ds(index, 1), :], (ROWS, LANES))

    def spread_columns(values, block, place):
        turned = values.T
        for tile in range(tiles):
            block[tile, place] = jnp.broadcast_to(turned[:, tile : tile + 1], (LANES, LANES))

    for component in range(3):
        spread_columns(window[component, home, :], columns, component)
    spread_columns(offset_own, columns, 3)

    lane = lax.broadcasted_iota(jnp.int32, (LANES, LANES), 1)

    def row_sums():
        gathered = jnp.zeros((LANES, LANES), jnp.float32)
        for tile in range(tiles):
            added = jnp.sum(sums[tile, 0], axis=1, keepdims=True)
            gathered = jnp.where(lane == tile, added, gathered)
        return gathered.T[:tiles, :]

    def born_near(tile, carry):
        partner = [row_of(window.at[c], 2 * tiles + tile) for c in (0, 1, 2, 4)]
        scaled_square = partner[3] * partner[3]
        for step in range(steps):
            rows = pl.ds(step * ROWS, ROWS)
            own = [columns[tile, c, rows, :] for c in range(4)]
            squared = squared_distance(own, partner)
            distances[tile, 0, rows, :] = squared
            terms = born_parts(
                squared, own[3], partner[3], scaled_square, diagonal_of(step * ROWS)
            )
            for place, term in enumerate(terms):
                sums[tile, place, rows, :] = term
        return carry

    lax.fori_loop(0, tiles, born_near, 0, unroll=2)
    wait_all(window, window_send, window_recv)

    def born_gather(tile, carry):
        for entry in range(1, width):
            index = lists[entry, tile]
            for place in range(3):
                partners[tile, entry, place] = row_of(window.at[place], index)
            scaled = jnp.where(entry < counts[tile], row_of(window.at[4], index), 0.0)
            partners[tile, entry, 3] = scaled
            partners[tile, entry, 4] = scaled * scaled
        return carry

    lax.fori_loop(0, tiles, born_gather, 0, unroll=4)

    def born_far(tile, carry):
        def one_step(step, inner):
            rows = pl.ds(pl.multiple_of(step * ROWS, ROWS), ROWS)
            own = [columns[tile, c, rows, :] for c in range(4)]
            totals = [sums[tile, c, rows, :] for c in range(3)]
            for entry in range(1, width):
                partner = [partners[tile, entry, c] for c in range(5)]
                squared = squared_distance(own, partner)
                distances[tile, entry, rows, :] = squared
                terms = born_parts(squared, own[3], partner[3], partner[4])
                totals = [old + term for old, term in zip(totals, terms)]
            sums[tile, 0, rows, :] = (
                0.125 * totals[0] + 0.25 * totals[1] + (2.0 / own[3]) * totals[2]
            )
            return inner

        lax.fori_loop(0, steps, one_step, 0, unroll=steps)
        return carry

    lax.fori_loop(0, tiles, born_far, 0)

    radius_own = jnp.where(live, radii[...], 1.5)
    psi = row_sums() * offset_own
    bending = jnp.tanh(psi - 0.8 * psi * psi + 4.85 * psi * psi * psi)
    born = 1.0 / (1.0 / offset_own - bending / radius_own)
    born_out[...] = jnp.where(live, born, 0.0)
    born_window[home, :] = jnp.where(live, born, 1.0)
    send_all(born_window, born_send, born_recv)

    own_over = 1.0 / born_window[home, :]
    over_window[home, :] = own_over
    charge_window[home, :] = window[3, home, :] * lax.rsqrt(born_window[home, :])
    spread_columns(own_over, born_columns, 0)

    def energy_near(tile, carry):
        partner = [row_of(buffer, 2 * tiles + tile) for buffer in (over_window, charge_window)]
        for step in range(steps):
            rows = pl.ds(step * ROWS, ROWS)
            sums[tile, 0, rows, :] = energy_part(
                distances[tile, 0, rows, :], born_columns[tile, 0, rows, :], *partner
            )
        return carry

    lax.fori_loop(0, tiles, energy_near, 0, unroll=4)
    wait_all(born_window, born_send, born_recv)
    over_window[...] = 1.0 / born_window[...]
    charge_window[...] = window[3] * lax.rsqrt(born_window[...])

    def energy_gather(tile, carry):
        for entry in range(1, width):
            index = lists[entry, tile]
            partners[tile, entry, 0] = row_of(over_window, index)
            partners[tile, entry, 1] = jnp.where(
                entry < counts[tile], row_of(charge_window, index), 0.0
            )
        return carry

    lax.fori_loop(0, tiles, energy_gather, 0, unroll=4)

    def energy_far(tile, carry):
        def one_step(step, inner):
            rows = pl.ds(pl.multiple_of(step * ROWS, ROWS), ROWS)
            own_column = born_columns[tile, 0, rows, :]
            total = sums[tile, 0, rows, :]
            for entry in range(1, width):
                total = total + energy_part(
                    distances[tile, entry, rows, :],
                    own_column,
                    partners[tile, entry, 0],
                    partners[tile, entry, 1],
                )
            sums[tile, 0, rows, :] = total
            return inner

        lax.fori_loop(0, steps, one_step, 0, unroll=steps)
        return carry

    lax.fori_loop(0, tiles, energy_far, 0)

    energy = -0.5 * charge_window[home, :] * row_sums()
    energy_out[...] = energy
    total_window[pl.ds(me, 1), :] = jnp.sum(energy, axis=0, keepdims=True)

    def total_copy(step):
        mine = total_window.at[pl.ds(me, 1), :]
        return pltpu.make_async_remote_copy(
            src_ref=mine,
            dst_ref=mine,
            send_sem=total_send.at[step],
            recv_sem=total_recv.at[step],
            device_id=(lax.rem(me + step, count),),
            device_id_type=MESH,
        )

    def total_start(step, carry):
        total_copy(step).start()
        return carry

    def total_wait(step, carry):
        total_copy(step).wait_recv()
        return carry

    def total_sent(step, carry):
        total_copy(step).wait_send()
        return carry

    lax.fori_loop(1, count, total_start, 0)
    lax.fori_loop(1, count, total_wait, 0)
    total_out[0, 0] = jnp.sum(total_window[...])
    lax.fori_loop(1, count, total_sent, 0)


def hand_over(born, energy, born_out, energy_out, sems):
    copies = [
        pltpu.make_async_copy(born, born_out, sems.at[0]),
        pltpu.make_async_copy(energy, energy_out, sems.at[1]),
    ]
    for copy in copies:
        copy.start()
    for copy in copies:
        copy.wait()


def solution(mesh):
    count = mesh.shape["slab"]

    def shards(coords, charges, radii, screens, tile_lists, tile_counts, slab_fill):
        tiles = charges.shape[0] // LANES
        width = tile_lists.shape[1]
        block = jax.ShapeDtypeStruct((tiles, LANES), jnp.float32)
        smem = pl.BlockSpec(memory_space=pltpu.SMEM)
        hbm = pl.BlockSpec(memory_space=pltpu.HBM)
        vmem = pl.BlockSpec(memory_space=pltpu.VMEM)
        born, energy, total = pl.pallas_call(
            functools.partial(kernel, count),
            out_shape=(block, block, jax.ShapeDtypeStruct((1, 1), jnp.float32)),
            in_specs=[hbm] * 7,
            out_specs=(vmem, vmem, smem),
            scratch_shapes=[
                pltpu.SMEM((width, tiles), jnp.int32),
                pltpu.SMEM((tiles,), jnp.int32),
                pltpu.SMEM((1,), jnp.int32),
                pltpu.VMEM(coords.shape, jnp.float32),
                pltpu.VMEM((tiles, LANES), jnp.float32),
                pltpu.VMEM((tiles, LANES), jnp.float32),
                pltpu.VMEM((tiles, LANES), jnp.float32),
                pltpu.VMEM((5, 5 * tiles, LANES), jnp.float32),
                pltpu.VMEM((5 * tiles, LANES), jnp.float32),
                pltpu.VMEM((5 * tiles, LANES), jnp.float32),
                pltpu.VMEM((5 * tiles, LANES), jnp.float32),
                pltpu.VMEM((count, LANES), jnp.float32),
                pltpu.VMEM((tiles, 4, LANES, LANES), jnp.float32),
                pltpu.VMEM((tiles, 1, LANES, LANES), jnp.float32),
                pltpu.VMEM((tiles, width, 5, ROWS, LANES), jnp.float32),
                pltpu.VMEM((tiles, 3, LANES, LANES), jnp.float32),
                pltpu.VMEM((tiles, width, LANES, LANES), jnp.float32),
                pltpu.SemaphoreType.DMA((7,)),
                pltpu.SemaphoreType.DMA((len(SHIFTS),)),
                pltpu.SemaphoreType.DMA((len(SHIFTS),)),
                pltpu.SemaphoreType.DMA((len(SHIFTS),)),
                pltpu.SemaphoreType.DMA((len(SHIFTS),)),
                pltpu.SemaphoreType.DMA((count,)),
                pltpu.SemaphoreType.DMA((count,)),
            ],
            compiler_params=pltpu.CompilerParams(
                collective_id=0, has_side_effects=True, vmem_limit_bytes=63463424

            ),
        )(
            tile_lists.T,
            tile_counts,
            slab_fill,
            coords,
            charges.reshape(tiles, LANES),
            radii.reshape(tiles, LANES),
            screens.reshape(tiles, LANES),
        )
        born, energy = pl.pallas_call(
            hand_over,
            out_shape=(block, block),
            in_specs=[hbm] * 2,
            out_specs=(hbm, hbm),
            scratch_shapes=[pltpu.SemaphoreType.DMA((2,))],
        )(born, energy)
        return born.reshape(-1), energy.reshape(-1), total.reshape(())

    placed = (
        P(None, "slab"),
        P("slab"),
        P("slab"),
        P("slab"),
        P("slab", None),
        P("slab"),
        P("slab"),
    )
    return jax.shard_map(
        shards, mesh=mesh, in_specs=placed, out_specs=(P("slab"), P("slab"), P()), check_vma=False
    )
```

```python
import functools

import jax
import jax.numpy as jnp
from jax import lax
from jax.experimental import pallas as pl
from jax.experimental.pallas import tpu as pltpu
from jax.sharding import PartitionSpec as P

OFFSET = 0.09
SOFTEN = 1.0
LOG2E = 1.4426950408889634
MESH = pl.DeviceIdType.MESH
SHIFTS = (1, -1, 2, -2)
LANES = 128
ROWS = 8


def softened_distance(own, partner):
    total = (own[3] + partner[3]) + own[0] * partner[0]
    return (total + own[1] * partner[1]) + own[2] * partner[2]


def born_parts(soft, offset_own, scaled, scaled_square, diagonal=None):
    inverse = lax.rsqrt(soft)
    distance = soft * inverse
    upper = distance + scaled
    reach = distance - scaled
    inner = jnp.maximum(offset_own, scaled - distance)
    lower = jnp.minimum(jnp.maximum(inner, reach), upper)
    both = pl.reciprocal(upper * lower, approx=True)
    over_lower = upper * both
    over_upper = lower * both
    apart = over_lower - over_upper
    bend = distance - scaled_square * inverse
    first = apart * (4.0 - bend * (over_lower + over_upper))
    second = inverse * jnp.log(lower * over_upper)
    third = (inner - offset_own) * over_lower
    if diagonal is not None:
        first = jnp.where(diagonal, 0.0, first)
        second = jnp.where(diagonal, 0.0, second)
        third = jnp.where(diagonal, 0.0, third)
    return first, second, third


def energy_part(soft, own_over, partner_over, partner_charge):
    scaled = (soft - SOFTEN) * (own_over * partner_over)
    return partner_charge * lax.rsqrt(scaled + jnp.exp2(scaled * (-0.25 * LOG2E)))


def kernel(
    count,
    lists_in,
    counts_in,
    fill_in,
    coords_in,
    charges_in,
    radii_in,
    screens_in,
    born_out,
    energy_out,
    total_out,
    lists,
    counts,
    fill,
    coords,
    charges,
    radii,
    screens,
    window,
    places,
    born_window,
    over_window,
    charge_window,
    total_window,
    columns,
    born_columns,
    partners,
    sums,
    distances,
    load_sems,
    window_send,
    window_recv,
    born_send,
    born_recv,
    total_send,
    total_recv,
):
    me = lax.axis_index("slab")
    tiles = charges.shape[0]
    width = lists.shape[0]
    steps = LANES // ROWS

    loads = [
        pltpu.make_async_copy(source, target, load_sems.at[place])
        for place, (source, target) in enumerate(
            (
                (fill_in, fill),
                (radii_in, radii),
                (screens_in, screens),
                (charges_in, charges),
                (coords_in, coords),
                (lists_in, lists),
                (counts_in, counts),
            )
        )
    ]
    for load in loads:
        load.start()

    barrier = pltpu.get_barrier_semaphore()

    def greet(step, carry):
        pl.semaphore_signal(
            barrier, inc=1, device_id=(lax.rem(me + step, count),), device_id_type=MESH
        )
        return carry

    lax.fori_loop(1, count, greet, 0)
    for load in loads:
        load.wait()

    slots = lax.broadcasted_iota(jnp.int32, (tiles, LANES), 0) * LANES
    slots = slots + lax.broadcasted_iota(jnp.int32, (tiles, LANES), 1)
    live = slots < fill[0]
    offset_own = jnp.where(live, radii[...] - OFFSET, 1.5 - OFFSET)
    home = pl.ds(2 * tiles, tiles)
    for component in range(3):
        for tile in range(tiles):
            window[component, 2 * tiles + tile : 2 * tiles + tile + 1, :] = coords[
                component : component + 1, tile * LANES : (tile + 1) * LANES
            ]
    window[3, home, :] = jnp.where(live, charges[...], 0.0)
    window[4, home, :] = jnp.where(live, screens[...] * (radii[...] - OFFSET), 0.0)

    def there(shift):
        return jnp.logical_and(me + shift >= 0, me + shift < count)

    def send(buffer, sems_out, sems_in, place, shift):
        def view(spot):
            rows = pl.ds(spot * tiles, tiles)
            return buffer.at[:, rows, :] if len(buffer.shape) == 3 else buffer.at[rows, :]

        return pltpu.make_async_remote_copy(
            src_ref=view(2),
            dst_ref=view(2 - shift),
            send_sem=sems_out.at[place],
            recv_sem=sems_in.at[place],
            device_id=(me + shift,),
            device_id_type=MESH,
        )

    def send_all(buffer, sems_out, sems_in):
        for place, shift in enumerate(SHIFTS):
            copy = send(buffer, sems_out, sems_in, place, shift)
            pl.when(there(shift))(copy.start)

    def wait_all(buffer, sems_out, sems_in):
        for place, shift in enumerate(SHIFTS):
            copy = send(buffer, sems_out, sems_in, place, shift)
            pl.when(there(shift))(copy.wait_send)
            pl.when(there(-shift))(copy.wait_recv)

    for shift in SHIFTS:

        @pl.when(jnp.logical_not(there(-shift)))
        def _():
            rows = pl.ds((2 - shift) * tiles, tiles)
            window[:, rows, :] = jnp.zeros((5, tiles, LANES), jnp.float32)
            born_window[rows, :] = jnp.ones((tiles, LANES), jnp.float32)

    pl.semaphore_wait(barrier, count - 1)
    send_all(window, window_send, window_recv)

    def diagonal_of(row):
        own_slot = lax.broadcasted_iota(jnp.int32, (ROWS, LANES), 0) + row
        return own_slot == lax.broadcasted_iota(jnp.int32, (ROWS, LANES), 1)

    def row_of(buffer, index):
        return jnp.broadcast_to(buffer[pl.ds(index, 1), :], (ROWS, LANES))

    def spread_columns(values, block, place):
        turned = values.T
        for tile in range(tiles):
            block[tile, place] = jnp.broadcast_to(turned[:, tile : tile + 1], (LANES, LANES))

    middle = 2 * tiles + tiles // 2
    centre = [window[c, middle : middle + 1, :1] for c in range(3)]

    def place_around(rows):
        length = jnp.zeros((rows.size, LANES), jnp.float32)
        for component in range(3):
            moved = window[component, rows, :] - centre[component]
            places[component, rows, :] = moved
            length = length + moved * moved
        places[3, rows, :] = length

    place_around(home)
    for component in range(3):
        spread_columns(-2.0 * places[component, home, :], columns, component)
    spread_columns(places[3, home, :] + SOFTEN, columns, 3)
    spread_columns(offset_own, columns, 4)

    lane = lax.broadcasted_iota(jnp.int32, (LANES, LANES), 1)

    def row_sums():
        gathered = jnp.zeros((LANES, LANES), jnp.float32)
        for tile in range(tiles):
            added = jnp.sum(sums[tile, 0], axis=1, keepdims=True)
            gathered = jnp.where(lane == tile, added, gathered)
        return gathered.T[:tiles, :]

    def born_near(tile, carry):
        partner = [row_of(places.at[c], 2 * tiles + tile) for c in range(4)]
        scaled = row_of(window.at[4], 2 * tiles + tile)
        scaled_square = scaled * scaled
        for step in range(steps):
            rows = pl.ds(step * ROWS, ROWS)
            own = [columns[tile, c, rows, :] for c in range(5)]
            diagonal = diagonal_of(step * ROWS)
            soft = jnp.where(diagonal, SOFTEN, softened_distance(own, partner))
            distances[tile, 0, rows, :] = soft
            terms = born_parts(soft, own[4], scaled, scaled_square, diagonal)
            for place, term in enumerate(terms):
                sums[tile, place, rows, :] = term
        return carry

    lax.fori_loop(0, tiles, born_near, 0)
    wait_all(window, window_send, window_recv)
    place_around(pl.ds(0, 2 * tiles))
    place_around(pl.ds(3 * tiles, 2 * tiles))

    def born_gather(tile, carry):
        for entry in range(1, width):
            index = lists[entry, tile]
            for place in range(4):
                partners[tile, entry, place] = row_of(places.at[place], index)
            scaled = jnp.where(entry < counts[tile], row_of(window.at[4], index), 0.0)
            partners[tile, entry, 4] = scaled
            partners[tile, entry, 5] = scaled * scaled
        return carry

    lax.fori_loop(0, tiles, born_gather, 0, unroll=4)

    def born_far(tile, carry):
        def one_step(step, inner):
            rows = pl.ds(pl.multiple_of(step * ROWS, ROWS), ROWS)
            own = [columns[tile, c, rows, :] for c in range(5)]
            totals = [sums[tile, c, rows, :] for c in range(3)]
            for entry in range(1, width):
                partner = [partners[tile, entry, c] for c in range(6)]
                soft = softened_distance(own, partner)
                distances[tile, entry, rows, :] = soft
                terms = born_parts(soft, own[4], partner[4], partner[5])
                totals = [old + term for old, term in zip(totals, terms)]
            sums[tile, 0, rows, :] = (
                0.125 * totals[0] + 0.25 * totals[1] + (2.0 / own[4]) * totals[2]
            )
            return inner

        lax.fori_loop(0, steps, one_step, 0, unroll=8)
        return carry

    lax.fori_loop(0, tiles, born_far, 0)

    radius_own = jnp.where(live, radii[...], 1.5)
    psi = row_sums() * offset_own
    bending = jnp.tanh(psi - 0.8 * psi * psi + 4.85 * psi * psi * psi)
    born = 1.0 / (1.0 / offset_own - bending / radius_own)
    born_out[...] = jnp.where(live, born, 0.0)
    born_window[home, :] = jnp.where(live, born, 1.0)
    send_all(born_window, born_send, born_recv)

    own_over = 1.0 / born_window[home, :]
    over_window[home, :] = own_over
    charge_window[home, :] = window[3, home, :] * lax.rsqrt(born_window[home, :])
    spread_columns(own_over, born_columns, 0)

    def energy_near(tile, carry):
        partner = [row_of(buffer, 2 * tiles + tile) for buffer in (over_window, charge_window)]
        for step in range(steps):
            rows = pl.ds(step * ROWS, ROWS)
            sums[tile, 0, rows, :] = energy_part(
                distances[tile, 0, rows, :], born_columns[tile, 0, rows, :], *partner
            )
        return carry

    lax.fori_loop(0, tiles, energy_near, 0)
    wait_all(born_window, born_send, born_recv)
    over_window[...] = 1.0 / born_window[...]
    charge_window[...] = window[3] * lax.rsqrt(born_window[...])

    def energy_gather(tile, carry):
        for entry in range(1, width):
            index = lists[entry, tile]
            partners[tile, entry, 0] = row_of(over_window, index)
            partners[tile, entry, 1] = jnp.where(
                entry < counts[tile], row_of(charge_window, index), 0.0
            )
        return carry

    lax.fori_loop(0, tiles, energy_gather, 0, unroll=4)

    def energy_far(tile, carry):
        def one_step(step, inner):
            rows = pl.ds(pl.multiple_of(step * ROWS, ROWS), ROWS)
            own_column = born_columns[tile, 0, rows, :]
            total = sums[tile, 0, rows, :]
            for entry in range(1, width):
                total = total + energy_part(
                    distances[tile, entry, rows, :],
                    own_column,
                    partners[tile, entry, 0],
                    partners[tile, entry, 1],
                )
            sums[tile, 0, rows, :] = total
            return inner

        lax.fori_loop(0, steps, one_step, 0, unroll=8)
        return carry

    lax.fori_loop(0, tiles, energy_far, 0)

    energy = -0.5 * charge_window[home, :] * row_sums()
    energy_out[...] = energy
    total_window[pl.ds(me, 1), :] = jnp.sum(energy, axis=0, keepdims=True)

    def total_copy(step):
        mine = total_window.at[pl.ds(me, 1), :]
        return pltpu.make_async_remote_copy(
            src_ref=mine,
            dst_ref=mine,
            send_sem=total_send.at[step],
            recv_sem=total_recv.at[step],
            device_id=(lax.rem(me + step, count),),
            device_id_type=MESH,
        )

    def total_start(step, carry):
        total_copy(step).start()
        return carry

    def total_wait(step, carry):
        total_copy(step).wait_recv()
        return carry

    def total_sent(step, carry):
        total_copy(step).wait_send()
        return carry

    lax.fori_loop(1, count, total_start, 0)
    lax.fori_loop(1, count, total_wait, 0)
    total_out[0, 0] = jnp.sum(total_window[...])
    lax.fori_loop(1, count, total_sent, 0)


def hand_over(born, energy, born_out, energy_out):
    born_out[...] = born[...]
    energy_out[...] = energy[...]


def solution(mesh):
    count = mesh.shape["slab"]

    def shards(coords, charges, radii, screens, tile_lists, tile_counts, slab_fill):
        tiles = charges.shape[0] // LANES
        width = tile_lists.shape[1]
        block = jax.ShapeDtypeStruct((tiles, LANES), jnp.float32)
        smem = pl.BlockSpec(memory_space=pltpu.SMEM)
        hbm = pl.BlockSpec(memory_space=pltpu.HBM)
        vmem = pl.BlockSpec(memory_space=pltpu.VMEM)
        born, energy, total = pl.pallas_call(
            functools.partial(kernel, count),
            out_shape=(block, block, jax.ShapeDtypeStruct((1, 1), jnp.float32)),
            in_specs=[hbm] * 7,
            out_specs=(vmem, vmem, smem),
            scratch_shapes=[
                pltpu.SMEM((width, tiles), jnp.int32),
                pltpu.SMEM((tiles,), jnp.int32),
                pltpu.SMEM((1,), jnp.int32),
                pltpu.VMEM(coords.shape, jnp.float32),
                pltpu.VMEM((tiles, LANES), jnp.float32),
                pltpu.VMEM((tiles, LANES), jnp.float32),
                pltpu.VMEM((tiles, LANES), jnp.float32),
                pltpu.VMEM((5, 5 * tiles, LANES), jnp.float32),
                pltpu.VMEM((4, 5 * tiles, LANES), jnp.float32),
                pltpu.VMEM((5 * tiles, LANES), jnp.float32),
                pltpu.VMEM((5 * tiles, LANES), jnp.float32),
                pltpu.VMEM((5 * tiles, LANES), jnp.float32),
                pltpu.VMEM((count, LANES), jnp.float32),
                pltpu.VMEM((tiles, 5, LANES, LANES), jnp.float32),
                pltpu.VMEM((tiles, 1, LANES, LANES), jnp.float32),
                pltpu.VMEM((tiles, width, 6, ROWS, LANES), jnp.float32),
                pltpu.VMEM((tiles, 3, LANES, LANES), jnp.float32),
                pltpu.VMEM((tiles, width, LANES, LANES), jnp.float32),
                pltpu.SemaphoreType.DMA((7,)),
                pltpu.SemaphoreType.DMA((len(SHIFTS),)),
                pltpu.SemaphoreType.DMA((len(SHIFTS),)),
                pltpu.SemaphoreType.DMA((len(SHIFTS),)),
                pltpu.SemaphoreType.DMA((len(SHIFTS),)),
                pltpu.SemaphoreType.DMA((count,)),
                pltpu.SemaphoreType.DMA((count,)),
            ],
            compiler_params=pltpu.CompilerParams(
                collective_id=0, has_side_effects=True, vmem_limit_bytes=63463424

            ),
        )(
            tile_lists.T,
            tile_counts,
            slab_fill,
            coords,
            charges.reshape(tiles, LANES),
            radii.reshape(tiles, LANES),
            screens.reshape(tiles, LANES),
        )
        born, energy = pl.pallas_call(
            hand_over,
            out_shape=(block, block),
            in_specs=[vmem] * 2,
            out_specs=(vmem, vmem),
        )(born, energy)
        return born.reshape(-1), energy.reshape(-1), total.reshape(())

    placed = (
        P(None, "slab"),
        P("slab"),
        P("slab"),
        P("slab"),
        P("slab", None),
        P("slab"),
        P("slab"),
    )
    return jax.shard_map(
        shards, mesh=mesh, in_specs=placed, out_specs=(P("slab"), P("slab"), P()), check_vma=False
    )
```

```python
import functools

import jax
import jax.numpy as jnp
from jax import lax
from jax.experimental import pallas as pl
from jax.experimental.pallas import tpu as pltpu
from jax.sharding import PartitionSpec as P

OFFSET = 0.09
SOFTEN = 1.0
LOG2E = 1.4426950408889634
MESH = pl.DeviceIdType.MESH
SHIFTS = (1, -1, 2, -2)
LANES = 128
ROWS = 8


def softened_distance(own, partner):
    total = (own[3] + partner[3]) + own[0] * partner[0]
    return (total + own[1] * partner[1]) + own[2] * partner[2]


def reciprocals(values):
    if len(values) == 1:
        return [pl.reciprocal(values[0], approx=True)]
    if len(values) == 2:
        both = pl.reciprocal(values[0] * values[1], approx=True)
        return [both * values[1], both * values[0]]
    if len(values) > 4:
        return reciprocals(values[:4]) + reciprocals(values[4:])
    pair = values[0] * values[1]
    rest = values[2] * values[3] if len(values) == 4 else values[2]
    whole = pl.reciprocal(pair * rest, approx=True)
    over_pair, over_rest = whole * rest, whole * pair
    first = [over_pair * values[1], over_pair * values[0]]
    if len(values) == 3:
        return first + [over_rest]
    return first + [over_rest * values[3], over_rest * values[2]]


def born_parts(softs, offsets, scaled, squares):
    shapes = []
    for soft, offset_own, radius in zip(softs, offsets, scaled):
        inverse = lax.rsqrt(soft)
        distance = soft * inverse
        upper = distance + radius
        inner = jnp.maximum(offset_own, radius - distance)
        lower = jnp.minimum(jnp.maximum(inner, distance - radius), upper)
        shapes.append((inverse, distance, upper, inner, lower))
    both = reciprocals([upper * lower for _, _, upper, _, lower in shapes])
    terms = []
    for (inverse, distance, upper, inner, lower), over, offset_own, square in zip(
        shapes, both, offsets, squares
    ):
        over_lower = upper * over
        over_upper = lower * over
        bend = distance - square * inverse
        first = (over_lower - over_upper) * (4.0 - bend * (over_lower + over_upper))
        second = inverse * jnp.log(lower * over_upper)
        third = (inner - offset_own) * over_lower
        terms.append((first, second, third))
    return terms


def energy_part(soft, own_over, partner_over, partner_charge):
    scaled = (soft - SOFTEN) * (own_over * partner_over)
    return partner_charge * lax.rsqrt(scaled + jnp.exp2(scaled * (-0.25 * LOG2E)))


def kernel(
    count,
    lists_in,
    counts_in,
    fill_in,
    coords_in,
    charges_in,
    radii_in,
    screens_in,
    born_out,
    energy_out,
    total_out,
    lists,
    counts,
    fill,
    coords,
    charges,
    radii,
    screens,
    window,
    places,
    born_window,
    over_window,
    charge_window,
    total_window,
    columns,
    born_columns,
    partners,
    sums,
    distances,
    load_sems,
    window_send,
    window_recv,
    born_send,
    born_recv,
    total_send,
    total_recv,
):
    me = lax.axis_index("slab")
    tiles = charges.shape[0]
    width = lists.shape[0]
    steps = LANES // ROWS

    loads = [
        pltpu.make_async_copy(source, target, load_sems.at[place])
        for place, (source, target) in enumerate(
            (
                (fill_in, fill),
                (radii_in, radii),
                (screens_in, screens),
                (charges_in, charges),
                (coords_in, coords),
                (lists_in, lists),
                (counts_in, counts),
            )
        )
    ]
    for load in loads:
        load.start()

    barrier = pltpu.get_barrier_semaphore()

    def greet(step, carry):
        pl.semaphore_signal(
            barrier, inc=1, device_id=(lax.rem(me + step, count),), device_id_type=MESH
        )
        return carry

    lax.fori_loop(1, count, greet, 0)
    for load in loads:
        load.wait()

    slots = lax.broadcasted_iota(jnp.int32, (tiles, LANES), 0) * LANES
    slots = slots + lax.broadcasted_iota(jnp.int32, (tiles, LANES), 1)
    live = slots < fill[0]
    offset_own = jnp.where(live, radii[...] - OFFSET, 1.5 - OFFSET)
    home = pl.ds(2 * tiles, tiles)
    for component in range(3):
        for tile in range(tiles):
            window[component, 2 * tiles + tile : 2 * tiles + tile + 1, :] = coords[
                component : component + 1, tile * LANES : (tile + 1) * LANES
            ]
    window[3, home, :] = jnp.where(live, charges[...], 0.0)
    window[4, home, :] = jnp.where(live, screens[...] * (radii[...] - OFFSET), 0.0)

    def there(shift):
        return jnp.logical_and(me + shift >= 0, me + shift < count)

    def send(buffer, sems_out, sems_in, place, shift):
        def view(spot):
            rows = pl.ds(spot * tiles, tiles)
            return buffer.at[:, rows, :] if len(buffer.shape) == 3 else buffer.at[rows, :]

        return pltpu.make_async_remote_copy(
            src_ref=view(2),
            dst_ref=view(2 - shift),
            send_sem=sems_out.at[place],
            recv_sem=sems_in.at[place],
            device_id=(me + shift,),
            device_id_type=MESH,
        )

    def send_all(buffer, sems_out, sems_in):
        for place, shift in enumerate(SHIFTS):
            copy = send(buffer, sems_out, sems_in, place, shift)
            pl.when(there(shift))(copy.start)

    def wait_all(buffer, sems_out, sems_in):
        for place, shift in enumerate(SHIFTS):
            copy = send(buffer, sems_out, sems_in, place, shift)
            pl.when(there(shift))(copy.wait_send)
            pl.when(there(-shift))(copy.wait_recv)

    for shift in SHIFTS:

        @pl.when(jnp.logical_not(there(-shift)))
        def _():
            rows = pl.ds((2 - shift) * tiles, tiles)
            window[:, rows, :] = jnp.zeros((5, tiles, LANES), jnp.float32)
            born_window[rows, :] = jnp.ones((tiles, LANES), jnp.float32)

    pl.semaphore_wait(barrier, count - 1)
    send_all(window, window_send, window_recv)

    def diagonal_of(row):
        own_slot = lax.broadcasted_iota(jnp.int32, (ROWS, LANES), 0) + row
        return own_slot == lax.broadcasted_iota(jnp.int32, (ROWS, LANES), 1)

    def row_of(buffer, index):
        return jnp.broadcast_to(buffer[pl.ds(index, 1), :], (ROWS, LANES))

    def spread_columns(values, block, place):
        turned = values.T
        for tile in range(tiles):
            block[tile, place] = jnp.broadcast_to(turned[:, tile : tile + 1], (LANES, LANES))

    middle = 2 * tiles + tiles // 2
    centre = [window[c, middle : middle + 1, :1] for c in range(3)]

    def place_around(rows):
        length = jnp.zeros((rows.size, LANES), jnp.float32)
        for component in range(3):
            moved = window[component, rows, :] - centre[component]
            places[component, rows, :] = moved
            length = length + moved * moved
        places[3, rows, :] = length

    place_around(home)
    for component in range(3):
        spread_columns(-2.0 * places[component, home, :], columns, component)
    spread_columns(places[3, home, :] + SOFTEN, columns, 3)
    spread_columns(offset_own, columns, 4)

    lane = lax.broadcasted_iota(jnp.int32, (LANES, LANES), 1)

    def row_sums():
        gathered = jnp.zeros((LANES, LANES), jnp.float32)
        for tile in range(tiles):
            added = jnp.sum(sums[tile, 0], axis=1, keepdims=True)
            gathered = jnp.where(lane == tile, added, gathered)
        return gathered.T[:tiles, :]

    def born_near(tile, carry):
        partner = [row_of(places.at[c], 2 * tiles + tile) for c in range(4)]
        scaled = row_of(window.at[4], 2 * tiles + tile)
        scaled_square = scaled * scaled
        for start in range(0, steps, 4):
            softs, offsets, marks = [], [], []
            for step in range(start, start + 4):
                rows = pl.ds(step * ROWS, ROWS)
                own = [columns[tile, c, rows, :] for c in range(5)]
                diagonal = diagonal_of(step * ROWS)
                soft = jnp.where(diagonal, SOFTEN, softened_distance(own, partner))
                distances[tile, 0, rows, :] = soft
                softs.append(soft)
                offsets.append(own[4])
                marks.append(diagonal)
            parts = born_parts(softs, offsets, [scaled] * 4, [scaled_square] * 4)
            for step, diagonal, terms in zip(range(start, start + 4), marks, parts):
                for place, term in enumerate(terms):
                    sums[tile, place, pl.ds(step * ROWS, ROWS), :] = jnp.where(diagonal, 0.0, term)
        return carry

    lax.fori_loop(0, tiles, born_near, 0)
    wait_all(window, window_send, window_recv)
    place_around(pl.ds(0, 2 * tiles))
    place_around(pl.ds(3 * tiles, 2 * tiles))

    def born_gather(tile, carry):
        for entry in range(1, width):
            index = lists[entry, tile]
            for place in range(4):
                partners[tile, entry, place] = row_of(places.at[place], index)
            scaled = jnp.where(entry < counts[tile], row_of(window.at[4], index), 0.0)
            partners[tile, entry, 4] = scaled
            partners[tile, entry, 5] = scaled * scaled
        return carry

    lax.fori_loop(0, tiles, born_gather, 0, unroll=4)

    def born_far(tile, carry):
        def one_step(step, inner):
            rows = pl.ds(pl.multiple_of(step * ROWS, ROWS), ROWS)
            own = [columns[tile, c, rows, :] for c in range(5)]
            totals = [sums[tile, c, rows, :] for c in range(3)]
            for first in range(1, width, 4):
                entries = range(first, min(first + 4, width))
                softs, scaled, squares = [], [], []
                for entry in entries:
                    partner = [partners[tile, entry, c] for c in range(6)]
                    soft = softened_distance(own, partner)
                    distances[tile, entry, rows, :] = soft
                    softs.append(soft)
                    scaled.append(partner[4])
                    squares.append(partner[5])
                for terms in born_parts(softs, [own[4]] * len(softs), scaled, squares):
                    totals = [old + term for old, term in zip(totals, terms)]
            sums[tile, 0, rows, :] = (
                0.125 * totals[0] + 0.25 * totals[1] + (2.0 / own[4]) * totals[2]
            )
            return inner

        lax.fori_loop(0, steps, one_step, 0, unroll=8)
        return carry

    lax.fori_loop(0, tiles, born_far, 0)

    radius_own = jnp.where(live, radii[...], 1.5)
    psi = row_sums() * offset_own
    bending = jnp.tanh(psi - 0.8 * psi * psi + 4.85 * psi * psi * psi)
    born = 1.0 / (1.0 / offset_own - bending / radius_own)
    born_out[...] = jnp.where(live, born, 0.0)
    born_window[home, :] = jnp.where(live, born, 1.0)
    send_all(born_window, born_send, born_recv)

    own_over = 1.0 / born_window[home, :]
    over_window[home, :] = own_over
    charge_window[home, :] = window[3, home, :] * lax.rsqrt(born_window[home, :])
    spread_columns(own_over, born_columns, 0)

    def energy_near(tile, carry):
        partner = [row_of(buffer, 2 * tiles + tile) for buffer in (over_window, charge_window)]
        for step in range(steps):
            rows = pl.ds(step * ROWS, ROWS)
            sums[tile, 0, rows, :] = energy_part(
                distances[tile, 0, rows, :], born_columns[tile, 0, rows, :], *partner
            )
        return carry

    lax.fori_loop(0, tiles, energy_near, 0)
    wait_all(born_window, born_send, born_recv)
    over_window[...] = 1.0 / born_window[...]
    charge_window[...] = window[3] * lax.rsqrt(born_window[...])

    def energy_gather(tile, carry):
        for entry in range(1, width):
            index = lists[entry, tile]
            partners[tile, entry, 0] = row_of(over_window, index)
            partners[tile, entry, 1] = jnp.where(
                entry < counts[tile], row_of(charge_window, index), 0.0
            )
        return carry

    lax.fori_loop(0, tiles, energy_gather, 0, unroll=4)

    def energy_far(tile, carry):
        def one_step(step, inner):
            rows = pl.ds(pl.multiple_of(step * ROWS, ROWS), ROWS)
            own_column = born_columns[tile, 0, rows, :]
            total = sums[tile, 0, rows, :]
            for entry in range(1, width):
                total = total + energy_part(
                    distances[tile, entry, rows, :],
                    own_column,
                    partners[tile, entry, 0],
                    partners[tile, entry, 1],
                )
            sums[tile, 0, rows, :] = total
            return inner

        lax.fori_loop(0, steps, one_step, 0, unroll=8)
        return carry

    lax.fori_loop(0, tiles, energy_far, 0)

    energy = -0.5 * charge_window[home, :] * row_sums()
    energy_out[...] = energy
    total_window[pl.ds(me, 1), :] = jnp.sum(energy, axis=0, keepdims=True)

    def total_copy(step):
        mine = total_window.at[pl.ds(me, 1), :]
        return pltpu.make_async_remote_copy(
            src_ref=mine,
            dst_ref=mine,
            send_sem=total_send.at[step],
            recv_sem=total_recv.at[step],
            device_id=(lax.rem(me + step, count),),
            device_id_type=MESH,
        )

    def total_start(step, carry):
        total_copy(step).start()
        return carry

    def total_wait(step, carry):
        total_copy(step).wait_recv()
        return carry

    def total_sent(step, carry):
        total_copy(step).wait_send()
        return carry

    lax.fori_loop(1, count, total_start, 0)
    lax.fori_loop(1, count, total_wait, 0)
    total_out[0, 0] = jnp.sum(total_window[...])
    lax.fori_loop(1, count, total_sent, 0)


def hand_over(born, energy, born_out, energy_out):
    born_out[...] = born[...]
    energy_out[...] = energy[...]


def solution(mesh):
    count = mesh.shape["slab"]

    def shards(coords, charges, radii, screens, tile_lists, tile_counts, slab_fill):
        tiles = charges.shape[0] // LANES
        width = tile_lists.shape[1]
        block = jax.ShapeDtypeStruct((tiles, LANES), jnp.float32)
        smem = pl.BlockSpec(memory_space=pltpu.SMEM)
        hbm = pl.BlockSpec(memory_space=pltpu.HBM)
        vmem = pl.BlockSpec(memory_space=pltpu.VMEM)
        born, energy, total = pl.pallas_call(
            functools.partial(kernel, count),
            out_shape=(block, block, jax.ShapeDtypeStruct((1, 1), jnp.float32)),
            in_specs=[hbm] * 7,
            out_specs=(vmem, vmem, smem),
            scratch_shapes=[
                pltpu.SMEM((width, tiles), jnp.int32),
                pltpu.SMEM((tiles,), jnp.int32),
                pltpu.SMEM((1,), jnp.int32),
                pltpu.VMEM(coords.shape, jnp.float32),
                pltpu.VMEM((tiles, LANES), jnp.float32),
                pltpu.VMEM((tiles, LANES), jnp.float32),
                pltpu.VMEM((tiles, LANES), jnp.float32),
                pltpu.VMEM((5, 5 * tiles, LANES), jnp.float32),
                pltpu.VMEM((4, 5 * tiles, LANES), jnp.float32),
                pltpu.VMEM((5 * tiles, LANES), jnp.float32),
                pltpu.VMEM((5 * tiles, LANES), jnp.float32),
                pltpu.VMEM((5 * tiles, LANES), jnp.float32),
                pltpu.VMEM((count, LANES), jnp.float32),
                pltpu.VMEM((tiles, 5, LANES, LANES), jnp.float32),
                pltpu.VMEM((tiles, 1, LANES, LANES), jnp.float32),
                pltpu.VMEM((tiles, width, 6, ROWS, LANES), jnp.float32),
                pltpu.VMEM((tiles, 3, LANES, LANES), jnp.float32),
                pltpu.VMEM((tiles, width, LANES, LANES), jnp.float32),
                pltpu.SemaphoreType.DMA((7,)),
                pltpu.SemaphoreType.DMA((len(SHIFTS),)),
                pltpu.SemaphoreType.DMA((len(SHIFTS),)),
                pltpu.SemaphoreType.DMA((len(SHIFTS),)),
                pltpu.SemaphoreType.DMA((len(SHIFTS),)),
                pltpu.SemaphoreType.DMA((count,)),
                pltpu.SemaphoreType.DMA((count,)),
            ],
            compiler_params=pltpu.CompilerParams(
                collective_id=0, has_side_effects=True, vmem_limit_bytes=63463424

            ),
        )(
            tile_lists.T,
            tile_counts,
            slab_fill,
            coords,
            charges.reshape(tiles, LANES),
            radii.reshape(tiles, LANES),
            screens.reshape(tiles, LANES),
        )
        born, energy = pl.pallas_call(
            hand_over,
            out_shape=(block, block),
            in_specs=[vmem] * 2,
            out_specs=(vmem, vmem),
        )(born, energy)
        return born.reshape(-1), energy.reshape(-1), total.reshape(())

    placed = (
        P(None, "slab"),
        P("slab"),
        P("slab"),
        P("slab"),
        P("slab", None),
        P("slab"),
        P("slab"),
    )
    return jax.shard_map(
        shards, mesh=mesh, in_specs=placed, out_specs=(P("slab"), P("slab"), P()), check_vma=False
    )
```

```python
import functools

import jax
import jax.numpy as jnp
from jax import lax
from jax.experimental import pallas as pl
from jax.experimental.pallas import tpu as pltpu
from jax.sharding import PartitionSpec as P

OFFSET = 0.09
SOFTEN = 1.0
LOG2E = 1.4426950408889634
MESH = pl.DeviceIdType.MESH
SHIFTS = (1, -1, 2, -2)
LANES = 128
ROWS = 8


def softened_distance(own, partner):
    total = (own[3] + partner[3]) + own[0] * partner[0]
    return (total + own[1] * partner[1]) + own[2] * partner[2]


def born_parts(soft, offset_own, scaled, scaled_square, diagonal=None):
    inverse = lax.rsqrt(soft)
    distance = soft * inverse
    upper = distance + scaled
    reach = distance - scaled
    inner = jnp.maximum(offset_own, scaled - distance)
    lower = jnp.minimum(jnp.maximum(inner, reach), upper)
    both = pl.reciprocal(upper * lower, approx=True)
    over_lower = upper * both
    over_upper = lower * both
    apart = over_lower - over_upper
    bend = distance - scaled_square * inverse
    first = apart * (4.0 - bend * (over_lower + over_upper))
    second = inverse * jnp.log(lower * over_upper)
    third = (inner - offset_own) * over_lower
    if diagonal is not None:
        first = jnp.where(diagonal, 0.0, first)
        second = jnp.where(diagonal, 0.0, second)
        third = jnp.where(diagonal, 0.0, third)
    return first, second, third


def energy_part(soft, own_over, partner_over, partner_charge):
    scaled = (soft - SOFTEN) * (own_over * partner_over)
    return partner_charge * lax.rsqrt(scaled + jnp.exp2(scaled * (-0.25 * LOG2E)))


def kernel(
    count,
    group,
    lists_in,
    counts_in,
    fill_in,
    coords_in,
    charges_in,
    radii_in,
    screens_in,
    born_out,
    energy_out,
    total_out,
    lists,
    counts,
    fill,
    coords,
    charges,
    radii,
    screens,
    window,
    places,
    born_window,
    over_window,
    charge_window,
    near_window,
    far_window,
    columns,
    born_columns,
    partners,
    sums,
    distances,
    load_sems,
    window_send,
    window_recv,
    born_send,
    born_recv,
    near_send,
    near_recv,
    far_send,
    far_recv,
):
    me = lax.axis_index("slab")
    tiles = charges.shape[0]
    width = lists.shape[0]
    steps = LANES // ROWS

    loads = [
        pltpu.make_async_copy(source, target, load_sems.at[place])
        for place, (source, target) in enumerate(
            (
                (fill_in, fill),
                (radii_in, radii),
                (screens_in, screens),
                (charges_in, charges),
                (coords_in, coords),
                (lists_in, lists),
                (counts_in, counts),
            )
        )
    ]
    for load in loads:
        load.start()

    barrier = pltpu.get_barrier_semaphore()

    def there(shift):
        return jnp.logical_and(me + shift >= 0, me + shift < count)

    def greet(device):
        pl.semaphore_signal(barrier, inc=1, device_id=(device,), device_id_type=MESH)

    rank = lax.rem(me, group)
    first = me - rank
    near_peers = [first + lax.rem(rank + step, group) for step in range(1, group)]
    far_peers = [lax.rem(me + step * group, count) for step in range(1, count // group)]
    for shift in SHIFTS:
        pl.when(there(shift))(functools.partial(greet, me + shift))
    for peer in near_peers + far_peers:
        greet(peer)
    for load in loads:
        load.wait()

    slots = lax.broadcasted_iota(jnp.int32, (tiles, LANES), 0) * LANES
    slots = slots + lax.broadcasted_iota(jnp.int32, (tiles, LANES), 1)
    live = slots < fill[0]
    offset_own = jnp.where(live, radii[...] - OFFSET, 1.5 - OFFSET)
    home = pl.ds(2 * tiles, tiles)
    for component in range(3):
        for tile in range(tiles):
            window[component, 2 * tiles + tile : 2 * tiles + tile + 1, :] = coords[
                component : component + 1, tile * LANES : (tile + 1) * LANES
            ]
    window[3, home, :] = jnp.where(live, charges[...], 0.0)
    window[4, home, :] = jnp.where(live, screens[...] * (radii[...] - OFFSET), 0.0)

    def send(buffer, sems_out, sems_in, place, shift):
        def view(spot):
            rows = pl.ds(spot * tiles, tiles)
            return buffer.at[:, rows, :] if len(buffer.shape) == 3 else buffer.at[rows, :]

        return pltpu.make_async_remote_copy(
            src_ref=view(2),
            dst_ref=view(2 - shift),
            send_sem=sems_out.at[place],
            recv_sem=sems_in.at[place],
            device_id=(me + shift,),
            device_id_type=MESH,
        )

    def send_all(buffer, sems_out, sems_in):
        for place, shift in enumerate(SHIFTS):
            copy = send(buffer, sems_out, sems_in, place, shift)
            pl.when(there(shift))(copy.start)

    def wait_all(buffer, sems_out, sems_in):
        for place, shift in enumerate(SHIFTS):
            copy = send(buffer, sems_out, sems_in, place, shift)
            pl.when(there(shift))(copy.wait_send)
            pl.when(there(-shift))(copy.wait_recv)

    for shift in SHIFTS:

        @pl.when(jnp.logical_not(there(-shift)))
        def _():
            rows = pl.ds((2 - shift) * tiles, tiles)
            window[:, rows, :] = jnp.zeros((5, tiles, LANES), jnp.float32)
            born_window[rows, :] = jnp.ones((tiles, LANES), jnp.float32)

    greetings = len(near_peers) + len(far_peers)
    for shift in SHIFTS:
        greetings = greetings + there(shift).astype(jnp.int32)
    pl.semaphore_wait(barrier, greetings)
    send_all(window, window_send, window_recv)

    def diagonal_of(row):
        own_slot = lax.broadcasted_iota(jnp.int32, (ROWS, LANES), 0) + row
        return own_slot == lax.broadcasted_iota(jnp.int32, (ROWS, LANES), 1)

    def row_of(buffer, index):
        return jnp.broadcast_to(buffer[pl.ds(index, 1), :], (ROWS, LANES))

    def spread_columns(values, block, place):
        turned = values.T
        for tile in range(tiles):
            block[tile, place] = jnp.broadcast_to(turned[:, tile : tile + 1], (LANES, LANES))

    middle = 2 * tiles + tiles // 2
    centre = [window[c, middle : middle + 1, :1] for c in range(3)]

    def place_around(rows):
        length = jnp.zeros((rows.size, LANES), jnp.float32)
        for component in range(3):
            moved = window[component, rows, :] - centre[component]
            places[component, rows, :] = moved
            length = length + moved * moved
        places[3, rows, :] = length

    place_around(home)
    for component in range(3):
        spread_columns(-2.0 * places[component, home, :], columns, component)
    spread_columns(places[3, home, :] + SOFTEN, columns, 3)
    spread_columns(offset_own, columns, 4)

    lane = lax.broadcasted_iota(jnp.int32, (LANES, LANES), 1)

    def row_sums():
        gathered = jnp.zeros((LANES, LANES), jnp.float32)
        for tile in range(tiles):
            added = jnp.sum(sums[tile, 0], axis=1, keepdims=True)
            gathered = jnp.where(lane == tile, added, gathered)
        return gathered.T[:tiles, :]

    def born_near(tile, carry):
        partner = [row_of(places.at[c], 2 * tiles + tile) for c in range(4)]
        scaled = row_of(window.at[4], 2 * tiles + tile)
        scaled_square = scaled * scaled
        for step in range(steps):
            rows = pl.ds(step * ROWS, ROWS)
            own = [columns[tile, c, rows, :] for c in range(5)]
            diagonal = diagonal_of(step * ROWS)
            soft = jnp.where(diagonal, SOFTEN, softened_distance(own, partner))
            distances[tile, 0, rows, :] = soft
            terms = born_parts(soft, own[4], scaled, scaled_square, diagonal)
            for place, term in enumerate(terms):
                sums[tile, place, rows, :] = term
        return carry

    lax.fori_loop(0, tiles, born_near, 0)
    wait_all(window, window_send, window_recv)
    place_around(pl.ds(0, 2 * tiles))
    place_around(pl.ds(3 * tiles, 2 * tiles))

    def born_gather(tile, carry):
        for entry in range(1, width):
            index = lists[entry, tile]
            for place in range(4):
                partners[tile, entry, place] = row_of(places.at[place], index)
            scaled = jnp.where(entry < counts[tile], row_of(window.at[4], index), 0.0)
            partners[tile, entry, 4] = scaled
            partners[tile, entry, 5] = scaled * scaled
        return carry

    lax.fori_loop(0, tiles, born_gather, 0, unroll=4)

    def born_far(tile, carry):
        def one_step(step, inner):
            rows = pl.ds(pl.multiple_of(step * ROWS, ROWS), ROWS)
            own = [columns[tile, c, rows, :] for c in range(5)]
            totals = [sums[tile, c, rows, :] for c in range(3)]
            for entry in range(1, width):
                partner = [partners[tile, entry, c] for c in range(6)]
                soft = softened_distance(own, partner)
                distances[tile, entry, rows, :] = soft
                terms = born_parts(soft, own[4], partner[4], partner[5])
                totals = [old + term for old, term in zip(totals, terms)]
            sums[tile, 0, rows, :] = (
                0.125 * totals[0] + 0.25 * totals[1] + (2.0 / own[4]) * totals[2]
            )
            return inner

        lax.fori_loop(0, steps, one_step, 0, unroll=steps)
        return carry

    lax.fori_loop(0, tiles, born_far, 0)

    radius_own = jnp.where(live, radii[...], 1.5)
    psi = row_sums() * offset_own
    bending = jnp.tanh(psi - 0.8 * psi * psi + 4.85 * psi * psi * psi)
    born = 1.0 / (1.0 / offset_own - bending / radius_own)
    born_out[...] = jnp.where(live, born, 0.0)
    born_window[home, :] = jnp.where(live, born, 1.0)
    send_all(born_window, born_send, born_recv)

    own_over = 1.0 / born_window[home, :]
    over_window[home, :] = own_over
    charge_window[home, :] = window[3, home, :] * lax.rsqrt(born_window[home, :])
    spread_columns(own_over, born_columns, 0)

    def energy_near(tile, carry):
        partner = [row_of(buffer, 2 * tiles + tile) for buffer in (over_window, charge_window)]
        for step in range(steps):
            rows = pl.ds(step * ROWS, ROWS)
            sums[tile, 0, rows, :] = energy_part(
                distances[tile, 0, rows, :], born_columns[tile, 0, rows, :], *partner
            )
        return carry

    lax.fori_loop(0, tiles, energy_near, 0)
    wait_all(born_window, born_send, born_recv)
    over_window[...] = 1.0 / born_window[...]
    charge_window[...] = window[3] * lax.rsqrt(born_window[...])

    def energy_gather(tile, carry):
        for entry in range(1, width):
            index = lists[entry, tile]
            partners[tile, entry, 0] = row_of(over_window, index)
            partners[tile, entry, 1] = jnp.where(
                entry < counts[tile], row_of(charge_window, index), 0.0
            )
        return carry

    lax.fori_loop(0, tiles, energy_gather, 0, unroll=4)

    def energy_far(tile, carry):
        def one_step(step, inner):
            rows = pl.ds(pl.multiple_of(step * ROWS, ROWS), ROWS)
            own_column = born_columns[tile, 0, rows, :]
            total = sums[tile, 0, rows, :]
            for entry in range(1, width):
                total = total + energy_part(
                    distances[tile, entry, rows, :],
                    own_column,
                    partners[tile, entry, 0],
                    partners[tile, entry, 1],
                )
            sums[tile, 0, rows, :] = total
            return inner

        lax.fori_loop(0, steps, one_step, 0, unroll=steps)
        return carry

    lax.fori_loop(0, tiles, energy_far, 0)

    energy = -0.5 * charge_window[home, :] * row_sums()
    energy_out[...] = energy

    def exchange(row, buffer, place, peers, sems_out, sems_in):
        mine = buffer.at[pl.ds(place, 1), :]
        buffer[pl.ds(place, 1), :] = row
        copies = [
            pltpu.make_async_remote_copy(
                src_ref=mine,
                dst_ref=mine,
                send_sem=sems_out.at[index],
                recv_sem=sems_in.at[index],
                device_id=(peer,),
                device_id_type=MESH,
            )
            for index, peer in enumerate(peers)
        ]
        for copy in copies:
            copy.start()
        for copy in copies:
            copy.wait_recv()
        return jnp.sum(buffer[...], axis=0, keepdims=True), copies

    row = jnp.sum(energy, axis=0, keepdims=True)
    row, near_copies = exchange(row, near_window, rank, near_peers, near_send, near_recv)
    row, far_copies = exchange(
        row, far_window, lax.div(me, group), far_peers, far_send, far_recv
    )
    total_out[0, 0] = jnp.sum(row)
    for copy in near_copies + far_copies:
        copy.wait_send()


def hand_over(born, energy, born_out, energy_out):
    born_out[...] = born[...]
    energy_out[...] = energy[...]


def solution(mesh):
    count = mesh.shape["slab"]
    group = next(size for size in range(1, count + 1) if count % size == 0 and size * size >= count)

    def shards(coords, charges, radii, screens, tile_lists, tile_counts, slab_fill):
        tiles = charges.shape[0] // LANES
        width = tile_lists.shape[1]
        block = jax.ShapeDtypeStruct((tiles, LANES), jnp.float32)
        smem = pl.BlockSpec(memory_space=pltpu.SMEM)
        hbm = pl.BlockSpec(memory_space=pltpu.HBM)
        vmem = pl.BlockSpec(memory_space=pltpu.VMEM)
        born, energy, total = pl.pallas_call(
            functools.partial(kernel, count, group),
            out_shape=(block, block, jax.ShapeDtypeStruct((1, 1), jnp.float32)),
            in_specs=[hbm] * 7,
            out_specs=(vmem, vmem, smem),
            scratch_shapes=[
                pltpu.SMEM((width, tiles), jnp.int32),
                pltpu.SMEM((tiles,), jnp.int32),
                pltpu.SMEM((1,), jnp.int32),
                pltpu.VMEM(coords.shape, jnp.float32),
                pltpu.VMEM((tiles, LANES), jnp.float32),
                pltpu.VMEM((tiles, LANES), jnp.float32),
                pltpu.VMEM((tiles, LANES), jnp.float32),
                pltpu.VMEM((5, 5 * tiles, LANES), jnp.float32),
                pltpu.VMEM((4, 5 * tiles, LANES), jnp.float32),
                pltpu.VMEM((5 * tiles, LANES), jnp.float32),
                pltpu.VMEM((5 * tiles, LANES), jnp.float32),
                pltpu.VMEM((5 * tiles, LANES), jnp.float32),
                pltpu.VMEM((group, LANES), jnp.float32),
                pltpu.VMEM((count // group, LANES), jnp.float32),
                pltpu.VMEM((tiles, 5, LANES, LANES), jnp.float32),
                pltpu.VMEM((tiles, 1, LANES, LANES), jnp.float32),
                pltpu.VMEM((tiles, width, 6, ROWS, LANES), jnp.float32),
                pltpu.VMEM((tiles, 3, LANES, LANES), jnp.float32),
                pltpu.VMEM((tiles, width, LANES, LANES), jnp.float32),
                pltpu.SemaphoreType.DMA((7,)),
                pltpu.SemaphoreType.DMA((len(SHIFTS),)),
                pltpu.SemaphoreType.DMA((len(SHIFTS),)),
                pltpu.SemaphoreType.DMA((len(SHIFTS),)),
                pltpu.SemaphoreType.DMA((len(SHIFTS),)),
                pltpu.SemaphoreType.DMA((group,)),
                pltpu.SemaphoreType.DMA((group,)),
                pltpu.SemaphoreType.DMA((count // group,)),
                pltpu.SemaphoreType.DMA((count // group,)),
            ],
            compiler_params=pltpu.CompilerParams(
                collective_id=0, has_side_effects=True, vmem_limit_bytes=63463424

            ),
        )(
            tile_lists.T,
            tile_counts,
            slab_fill,
            coords,
            charges.reshape(tiles, LANES),
            radii.reshape(tiles, LANES),
            screens.reshape(tiles, LANES),
        )
        born, energy = pl.pallas_call(
            hand_over,
            out_shape=(block, block),
            in_specs=[vmem] * 2,
            out_specs=(vmem, vmem),
        )(born, energy)
        return born.reshape(-1), energy.reshape(-1), total.reshape(())

    placed = (
        P(None, "slab"),
        P("slab"),
        P("slab"),
        P("slab"),
        P("slab", None),
        P("slab"),
        P("slab"),
    )
    return jax.shard_map(
        shards, mesh=mesh, in_specs=placed, out_specs=(P("slab"), P("slab"), P()), check_vma=False
    )
```

```python
import functools

import jax
import jax.numpy as jnp
from jax import lax
from jax.experimental import pallas as pl
from jax.experimental.pallas import tpu as pltpu
from jax.sharding import PartitionSpec as P

OFFSET = 0.09
SOFTEN = 1.0
LOG2E = 1.4426950408889634
MESH = pl.DeviceIdType.MESH
SHIFTS = (1, -1, 2, -2)
LANES = 128
ROWS = 8


def squared_distance(own, partner):
    dx = own[0] - partner[0]
    dy = own[1] - partner[1]
    dz = own[2] - partner[2]
    return dx * dx + dy * dy + dz * dz


def born_parts(squared, offset_own, scaled, diagonal=None):
    soft = squared + SOFTEN
    inverse = lax.rsqrt(soft)
    distance = soft * inverse
    upper = distance + scaled
    reach = distance - scaled
    inner = jnp.maximum(offset_own, scaled - distance)
    lower = jnp.minimum(jnp.maximum(inner, reach), upper)
    both = pl.reciprocal(upper * lower, approx=True)
    over_lower = upper * both
    over_upper = lower * both
    apart = over_lower - over_upper
    bend = distance - scaled * scaled * inverse
    first = apart * (4.0 - bend * (over_lower + over_upper))
    second = inverse * jnp.log(lower * over_upper)
    third = (inner - offset_own) * over_lower
    if diagonal is not None:
        first = jnp.where(diagonal, 0.0, first)
        second = jnp.where(diagonal, 0.0, second)
        third = jnp.where(diagonal, 0.0, third)
    return first, second, third


def energy_part(squared, own_over, partner_over, partner_charge):
    scaled = squared * (own_over * partner_over)
    return partner_charge * lax.rsqrt(scaled + jnp.exp2(scaled * (-0.25 * LOG2E)))


def kernel(
    count,
    lists_in,
    counts_in,
    fill_in,
    coords_in,
    charges_in,
    radii_in,
    screens_in,
    born_out,
    energy_out,
    total_out,
    lists,
    counts,
    fill,
    coords,
    charges,
    radii,
    screens,
    window,
    born_window,
    over_window,
    charge_window,
    total_window,
    columns,
    born_columns,
    partners,
    sums,
    distances,
    load_sems,
    window_send,
    window_recv,
    born_send,
    born_recv,
    total_send,
    total_recv,
):
    me = lax.axis_index("slab")
    tiles = charges.shape[0]
    width = lists.shape[0]
    steps = LANES // ROWS

    loads = [
        pltpu.make_async_copy(source, target, load_sems.at[place])
        for place, (source, target) in enumerate(
            (
                (fill_in, fill),
                (radii_in, radii),
                (screens_in, screens),
                (charges_in, charges),
                (coords_in, coords),
                (lists_in, lists),
                (counts_in, counts),
            )
        )
    ]
    for load in loads:
        load.start()

    barrier = pltpu.get_barrier_semaphore()

    def greet(step, carry):
        pl.semaphore_signal(
            barrier, inc=1, device_id=(lax.rem(me + step, count),), device_id_type=MESH
        )
        return carry

    lax.fori_loop(1, count, greet, 0)
    for load in loads:
        load.wait()

    slots = lax.broadcasted_iota(jnp.int32, (tiles, LANES), 0) * LANES
    slots = slots + lax.broadcasted_iota(jnp.int32, (tiles, LANES), 1)
    live = slots < fill[0]
    offset_own = jnp.where(live, radii[...] - OFFSET, 1.5 - OFFSET)
    home = pl.ds(2 * tiles, tiles)
    for component in range(3):
        for tile in range(tiles):
            window[component, 2 * tiles + tile : 2 * tiles + tile + 1, :] = coords[
                component : component + 1, tile * LANES : (tile + 1) * LANES
            ]
    window[3, home, :] = jnp.where(live, charges[...], 0.0)
    window[4, home, :] = jnp.where(live, screens[...] * (radii[...] - OFFSET), 0.0)

    def there(shift):
        return jnp.logical_and(me + shift >= 0, me + shift < count)

    def send(buffer, sems_out, sems_in, place, shift):
        def view(spot):
            rows = pl.ds(spot * tiles, tiles)
            return buffer.at[:, rows, :] if len(buffer.shape) == 3 else buffer.at[rows, :]

        return pltpu.make_async_remote_copy(
            src_ref=view(2),
            dst_ref=view(2 - shift),
            send_sem=sems_out.at[place],
            recv_sem=sems_in.at[place],
            device_id=(me + shift,),
            device_id_type=MESH,
        )

    def send_all(buffer, sems_out, sems_in):
        for place, shift in enumerate(SHIFTS):
            copy = send(buffer, sems_out, sems_in, place, shift)
            pl.when(there(shift))(copy.start)

    def wait_all(buffer, sems_out, sems_in):
        for place, shift in enumerate(SHIFTS):
            copy = send(buffer, sems_out, sems_in, place, shift)
            pl.when(there(shift))(copy.wait_send)
            pl.when(there(-shift))(copy.wait_recv)

    for shift in SHIFTS:

        @pl.when(jnp.logical_not(there(-shift)))
        def _():
            rows = pl.ds((2 - shift) * tiles, tiles)
            window[:, rows, :] = jnp.zeros((5, tiles, LANES), jnp.float32)
            born_window[rows, :] = jnp.ones((tiles, LANES), jnp.float32)

    pl.semaphore_wait(barrier, count - 1)
    send_all(window, window_send, window_recv)

    def diagonal_of(row):
        own_slot = lax.broadcasted_iota(jnp.int32, (ROWS, LANES), 0) + row
        return own_slot == lax.broadcasted_iota(jnp.int32, (ROWS, LANES), 1)

    def row_of(buffer, index):
        return jnp.broadcast_to(buffer[pl.ds(index, 1), :], (ROWS, LANES))

    def spread_columns(values, block, place):
        turned = values.T
        for tile in range(tiles):
            block[tile, place] = jnp.broadcast_to(turned[:, tile : tile + 1], (LANES, LANES))

    for component in range(3):
        spread_columns(window[component, home, :], columns, component)
    spread_columns(offset_own, columns, 3)

    lane = lax.broadcasted_iota(jnp.int32, (LANES, LANES), 1)

    def row_sums():
        gathered = jnp.zeros((LANES, LANES), jnp.float32)
        for tile in range(tiles):
            added = jnp.sum(sums[tile, 0], axis=1, keepdims=True)
            gathered = jnp.where(lane == tile, added, gathered)
        return gathered.T[:tiles, :]

    def born_near(tile, carry):
        partner = [row_of(window.at[c], 2 * tiles + tile) for c in (0, 1, 2, 4)]
        for step in range(steps):
            rows = pl.ds(step * ROWS, ROWS)
            own = [columns[tile, c, rows, :] for c in range(4)]
            squared = squared_distance(own, partner)
            distances[tile, 0, rows, :] = squared
            terms = born_parts(squared, own[3], partner[3], diagonal_of(step * ROWS))
            for place, term in enumerate(terms):
                sums[tile, place, rows, :] = term
        return carry

    lax.fori_loop(0, tiles, born_near, 0)
    wait_all(window, window_send, window_recv)

    def born_far(tile, carry):
        for entry in range(1, width):
            index = lists[entry, tile]
            for place in range(3):
                partners[entry, place] = row_of(window.at[place], index)
            partners[entry, 3] = jnp.where(entry < counts[tile], row_of(window.at[4], index), 0.0)

        def one_step(step, inner):
            spots = [pl.ds((step * 4 + part) * ROWS, ROWS) for part in range(4)]
            owns = [[columns[tile, c, rows, :] for c in range(4)] for rows in spots]
            totals = [[sums[tile, c, rows, :] for c in range(3)] for rows in spots]
            for entry in range(1, width):
                partner = [partners[entry, c] for c in range(4)]
                for part, (rows, own) in enumerate(zip(spots, owns)):
                    squared = squared_distance(own, partner)
                    distances[tile, entry, rows, :] = squared
                    terms = born_parts(squared, own[3], partner[3])
                    totals[part] = [old + term for old, term in zip(totals[part], terms)]
            for rows, own, total in zip(spots, owns, totals):
                sums[tile, 0, rows, :] = (
                    0.125 * total[0] + 0.25 * total[1] + (2.0 / own[3]) * total[2]
                )
            return inner

        lax.fori_loop(0, steps // 4, one_step, 0, unroll=steps // 4)
        return carry

    lax.fori_loop(0, tiles, born_far, 0)

    radius_own = jnp.where(live, radii[...], 1.5)
    psi = row_sums() * offset_own
    bending = jnp.tanh(psi - 0.8 * psi * psi + 4.85 * psi * psi * psi)
    born = 1.0 / (1.0 / offset_own - bending / radius_own)
    born_out[...] = jnp.where(live, born, 0.0)
    born_window[home, :] = jnp.where(live, born, 1.0)
    send_all(born_window, born_send, born_recv)

    own_over = 1.0 / born_window[home, :]
    over_window[home, :] = own_over
    charge_window[home, :] = window[3, home, :] * lax.rsqrt(born_window[home, :])
    spread_columns(own_over, born_columns, 0)

    def energy_near(tile, carry):
        partner = [row_of(buffer, 2 * tiles + tile) for buffer in (over_window, charge_window)]
        for step in range(steps):
            rows = pl.ds(step * ROWS, ROWS)
            sums[tile, 0, rows, :] = energy_part(
                distances[tile, 0, rows, :], born_columns[tile, 0, rows, :], *partner
            )
        return carry

    lax.fori_loop(0, tiles, energy_near, 0)
    wait_all(born_window, born_send, born_recv)
    over_window[...] = 1.0 / born_window[...]
    charge_window[...] = window[3] * lax.rsqrt(born_window[...])

    def energy_far(tile, carry):
        for entry in range(1, width):
            index = lists[entry, tile]
            partners[entry, 0] = row_of(over_window, index)
            partners[entry, 1] = jnp.where(
                entry < counts[tile], row_of(charge_window, index), 0.0
            )

        def one_step(step, inner):
            spots = [pl.ds((step * 4 + part) * ROWS, ROWS) for part in range(4)]
            own_columns = [born_columns[tile, 0, rows, :] for rows in spots]
            totals = [sums[tile, 0, rows, :] for rows in spots]
            for entry in range(1, width):
                over, charge = partners[entry, 0], partners[entry, 1]
                for part, rows in enumerate(spots):
                    totals[part] = totals[part] + energy_part(
                        distances[tile, entry, rows, :], own_columns[part], over, charge
                    )
            for rows, total in zip(spots, totals):
                sums[tile, 0, rows, :] = total
            return inner

        lax.fori_loop(0, steps // 4, one_step, 0, unroll=steps // 4)
        return carry

    lax.fori_loop(0, tiles, energy_far, 0)

    energy = -0.5 * charge_window[home, :] * row_sums()
    energy_out[...] = energy
    total_window[pl.ds(me, 1), :] = jnp.sum(energy, axis=0, keepdims=True)

    def total_copy(step):
        mine = total_window.at[pl.ds(me, 1), :]
        return pltpu.make_async_remote_copy(
            src_ref=mine,
            dst_ref=mine,
            send_sem=total_send.at[step],
            recv_sem=total_recv.at[step],
            device_id=(lax.rem(me + step, count),),
            device_id_type=MESH,
        )

    def total_start(step, carry):
        total_copy(step).start()
        return carry

    def total_wait(step, carry):
        total_copy(step).wait_recv()
        return carry

    def total_sent(step, carry):
        total_copy(step).wait_send()
        return carry

    lax.fori_loop(1, count, total_start, 0)
    lax.fori_loop(1, count, total_wait, 0)
    total_out[0, 0] = jnp.sum(total_window[...])
    lax.fori_loop(1, count, total_sent, 0)


def hand_over(born, energy, born_out, energy_out):
    born_out[...] = born[...]
    energy_out[...] = energy[...]


def solution(mesh):
    count = mesh.shape["slab"]

    def shards(coords, charges, radii, screens, tile_lists, tile_counts, slab_fill):
        tiles = charges.shape[0] // LANES
        width = tile_lists.shape[1]
        block = jax.ShapeDtypeStruct((tiles, LANES), jnp.float32)
        smem = pl.BlockSpec(memory_space=pltpu.SMEM)
        hbm = pl.BlockSpec(memory_space=pltpu.HBM)
        vmem = pl.BlockSpec(memory_space=pltpu.VMEM)
        born, energy, total = pl.pallas_call(
            functools.partial(kernel, count),
            out_shape=(block, block, jax.ShapeDtypeStruct((1, 1), jnp.float32)),
            in_specs=[hbm] * 7,
            out_specs=(vmem, vmem, smem),
            scratch_shapes=[
                pltpu.SMEM((width, tiles), jnp.int32),
                pltpu.SMEM((tiles,), jnp.int32),
                pltpu.SMEM((1,), jnp.int32),
                pltpu.VMEM(coords.shape, jnp.float32),
                pltpu.VMEM((tiles, LANES), jnp.float32),
                pltpu.VMEM((tiles, LANES), jnp.float32),
                pltpu.VMEM((tiles, LANES), jnp.float32),
                pltpu.VMEM((5, 5 * tiles, LANES), jnp.float32),
                pltpu.VMEM((5 * tiles, LANES), jnp.float32),
                pltpu.VMEM((5 * tiles, LANES), jnp.float32),
                pltpu.VMEM((5 * tiles, LANES), jnp.float32),
                pltpu.VMEM((count, LANES), jnp.float32),
                pltpu.VMEM((tiles, 4, LANES, LANES), jnp.float32),
                pltpu.VMEM((tiles, 1, LANES, LANES), jnp.float32),
                pltpu.VMEM((width, 4, ROWS, LANES), jnp.float32),
                pltpu.VMEM((tiles, 3, LANES, LANES), jnp.float32),
                pltpu.VMEM((tiles, width, LANES, LANES), jnp.float32),
                pltpu.SemaphoreType.DMA((7,)),
                pltpu.SemaphoreType.DMA((len(SHIFTS),)),
                pltpu.SemaphoreType.DMA((len(SHIFTS),)),
                pltpu.SemaphoreType.DMA((len(SHIFTS),)),
                pltpu.SemaphoreType.DMA((len(SHIFTS),)),
                pltpu.SemaphoreType.DMA((count,)),
                pltpu.SemaphoreType.DMA((count,)),
            ],
            compiler_params=pltpu.CompilerParams(
                collective_id=0, has_side_effects=True, vmem_limit_bytes=63463424

            ),
        )(
            tile_lists.T,
            tile_counts,
            slab_fill,
            coords,
            charges.reshape(tiles, LANES),
            radii.reshape(tiles, LANES),
            screens.reshape(tiles, LANES),
        )
        born, energy = pl.pallas_call(
            hand_over, out_shape=(block, block), in_specs=[vmem] * 2, out_specs=(vmem, vmem)
        )(born, energy)
        return born.reshape(-1), energy.reshape(-1), total.reshape(())

    placed = (
        P(None, "slab"),
        P("slab"),
        P("slab"),
        P("slab"),
        P("slab", None),
        P("slab"),
        P("slab"),
    )
    return jax.shard_map(
        shards, mesh=mesh, in_specs=placed, out_specs=(P("slab"), P("slab"), P()), check_vma=False
    )
```

```python
import functools

import jax
import jax.numpy as jnp
from jax import lax
from jax.experimental import pallas as pl
from jax.experimental.pallas import tpu as pltpu
from jax.sharding import PartitionSpec as P

OFFSET = 0.09
SOFTEN = 1.0
LOG2E = 1.4426950408889634
MESH = pl.DeviceIdType.MESH
SHIFTS = (1, -1, 2, -2)
LANES = 128
ROWS = 8


def squared_distance(own, partner):
    dx = own[0] - partner[0]
    dy = own[1] - partner[1]
    dz = own[2] - partner[2]
    return dx * dx + dy * dy + dz * dz


def born_parts(squared, offset_own, scaled, scaled_square, diagonal=None):
    soft = squared + SOFTEN
    inverse = lax.rsqrt(soft)
    distance = soft * inverse
    upper = distance + scaled
    reach = distance - scaled
    inner = jnp.maximum(offset_own, scaled - distance)
    lower = jnp.minimum(jnp.maximum(inner, reach), upper)
    both = pl.reciprocal(upper * lower, approx=True)
    over_lower = upper * both
    over_upper = lower * both
    apart = over_lower - over_upper
    bend = distance - scaled_square * inverse
    first = apart * (4.0 - bend * (over_lower + over_upper))
    second = inverse * jnp.log(lower * over_upper)
    third = (inner - offset_own) * over_lower
    if diagonal is not None:
        first = jnp.where(diagonal, 0.0, first)
        second = jnp.where(diagonal, 0.0, second)
        third = jnp.where(diagonal, 0.0, third)
    return first, second, third


def energy_part(squared, own_over, partner_over, partner_charge):
    scaled = squared * (own_over * partner_over)
    return partner_charge * lax.rsqrt(scaled + jnp.exp2(scaled * (-0.25 * LOG2E)))


def kernel(
    count,
    lists_in,
    counts_in,
    fill_in,
    coords_in,
    charges_in,
    radii_in,
    screens_in,
    born_out,
    energy_out,
    total_out,
    lists,
    counts,
    fill,
    coords,
    charges,
    radii,
    screens,
    window,
    born_window,
    over_window,
    charge_window,
    total_window,
    columns,
    born_columns,
    partners,
    sums,
    distances,
    load_sems,
    window_send,
    window_recv,
    born_send,
    born_recv,
    total_send,
    total_recv,
):
    me = lax.axis_index("slab")
    tiles = charges.shape[0]
    width = lists.shape[0]
    steps = LANES // ROWS

    loads = [
        pltpu.make_async_copy(source, target, load_sems.at[place])
        for place, (source, target) in enumerate(
            (
                (fill_in, fill),
                (radii_in, radii),
                (screens_in, screens),
                (charges_in, charges),
                (coords_in, coords),
                (lists_in, lists),
                (counts_in, counts),
            )
        )
    ]
    for load in loads:
        load.start()

    barrier = pltpu.get_barrier_semaphore()

    def greet(step, carry):
        pl.semaphore_signal(
            barrier, inc=1, device_id=(lax.rem(me + step, count),), device_id_type=MESH
        )
        return carry

    lax.fori_loop(1, count, greet, 0)
    for load in loads:
        load.wait()

    slots = lax.broadcasted_iota(jnp.int32, (tiles, LANES), 0) * LANES
    slots = slots + lax.broadcasted_iota(jnp.int32, (tiles, LANES), 1)
    live = slots < fill[0]
    offset_own = jnp.where(live, radii[...] - OFFSET, 1.5 - OFFSET)
    home = pl.ds(2 * tiles, tiles)
    for component in range(3):
        for tile in range(tiles):
            window[component, 2 * tiles + tile : 2 * tiles + tile + 1, :] = coords[
                component : component + 1, tile * LANES : (tile + 1) * LANES
            ]
    window[3, home, :] = jnp.where(live, charges[...], 0.0)
    window[4, home, :] = jnp.where(live, screens[...] * (radii[...] - OFFSET), 0.0)

    def there(shift):
        return jnp.logical_and(me + shift >= 0, me + shift < count)

    def send(buffer, sems_out, sems_in, place, shift):
        def view(spot):
            rows = pl.ds(spot * tiles, tiles)
            return buffer.at[:, rows, :] if len(buffer.shape) == 3 else buffer.at[rows, :]

        return pltpu.make_async_remote_copy(
            src_ref=view(2),
            dst_ref=view(2 - shift),
            send_sem=sems_out.at[place],
            recv_sem=sems_in.at[place],
            device_id=(me + shift,),
            device_id_type=MESH,
        )

    def send_all(buffer, sems_out, sems_in):
        for place, shift in enumerate(SHIFTS):
            copy = send(buffer, sems_out, sems_in, place, shift)
            pl.when(there(shift))(copy.start)

    def wait_all(buffer, sems_out, sems_in):
        for place, shift in enumerate(SHIFTS):
            copy = send(buffer, sems_out, sems_in, place, shift)
            pl.when(there(shift))(copy.wait_send)
            pl.when(there(-shift))(copy.wait_recv)

    for shift in SHIFTS:

        @pl.when(jnp.logical_not(there(-shift)))
        def _():
            rows = pl.ds((2 - shift) * tiles, tiles)
            window[:, rows, :] = jnp.zeros((5, tiles, LANES), jnp.float32)
            born_window[rows, :] = jnp.ones((tiles, LANES), jnp.float32)

    pl.semaphore_wait(barrier, count - 1)
    send_all(window, window_send, window_recv)

    def diagonal_of(row):
        own_slot = lax.broadcasted_iota(jnp.int32, (ROWS, LANES), 0) + row
        return own_slot == lax.broadcasted_iota(jnp.int32, (ROWS, LANES), 1)

    def row_of(buffer, index):
        return jnp.broadcast_to(buffer[pl.ds(index, 1), :], (ROWS, LANES))

    def spread_columns(values, block, place):
        turned = values.T
        for tile in range(tiles):
            block[tile, place] = jnp.broadcast_to(turned[:, tile : tile + 1], (LANES, LANES))

    for component in range(3):
        spread_columns(window[component, home, :], columns, component)
    spread_columns(offset_own, columns, 3)

    lane = lax.broadcasted_iota(jnp.int32, (LANES, LANES), 1)

    def row_sums():
        gathered = jnp.zeros((LANES, LANES), jnp.float32)
        for tile in range(tiles):
            added = jnp.sum(sums[tile, 0], axis=1, keepdims=True)
            gathered = jnp.where(lane == tile, added, gathered)
        return gathered.T[:tiles, :]

    def born_near(tile, carry):
        partner = [row_of(window.at[c], 2 * tiles + tile) for c in (0, 1, 2, 4)]
        scaled_square = partner[3] * partner[3]
        for step in range(steps):
            rows = pl.ds(step * ROWS, ROWS)
            own = [columns[tile, c, rows, :] for c in range(4)]
            squared = squared_distance(own, partner)
            distances[tile, 0, rows, :] = squared
            terms = born_parts(
                squared, own[3], partner[3], scaled_square, diagonal_of(step * ROWS)
            )
            for place, term in enumerate(terms):
                sums[tile, place, rows, :] = term
        return carry

    lax.fori_loop(0, tiles, born_near, 0, unroll=2)
    wait_all(window, window_send, window_recv)

    def born_gather(tile, carry):
        for entry in range(1, width):
            index = lists[entry, tile]
            for place in range(3):
                partners[tile, entry, place] = row_of(window.at[place], index)
            scaled = jnp.where(entry < counts[tile], row_of(window.at[4], index), 0.0)
            partners[tile, entry, 3] = scaled
            partners[tile, entry, 4] = scaled * scaled
        return carry

    lax.fori_loop(0, tiles, born_gather, 0, unroll=4)

    def born_far(tile, carry):
        def one_step(step, inner):
            rows = pl.ds(pl.multiple_of(step * ROWS, ROWS), ROWS)
            own = [columns[tile, c, rows, :] for c in range(4)]
            totals = [sums[tile, c, rows, :] for c in range(3)]
            for entry in range(1, width):
                partner = [partners[tile, entry, c] for c in range(5)]
                squared = squared_distance(own, partner)
                distances[tile, entry, rows, :] = squared
                terms = born_parts(squared, own[3], partner[3], partner[4])
                totals = [old + term for old, term in zip(totals, terms)]
            sums[tile, 0, rows, :] = (
                0.125 * totals[0] + 0.25 * totals[1] + (2.0 / own[3]) * totals[2]
            )
            return inner

        lax.fori_loop(0, steps, one_step, 0, unroll=steps)
        return carry

    lax.fori_loop(0, tiles, born_far, 0, unroll=2)

    radius_own = jnp.where(live, radii[...], 1.5)
    psi = row_sums() * offset_own
    bending = jnp.tanh(psi - 0.8 * psi * psi + 4.85 * psi * psi * psi)
    born = 1.0 / (1.0 / offset_own - bending / radius_own)
    born_out[...] = jnp.where(live, born, 0.0)
    born_window[home, :] = jnp.where(live, born, 1.0)
    send_all(born_window, born_send, born_recv)

    own_over = 1.0 / born_window[home, :]
    over_window[home, :] = own_over
    charge_window[home, :] = window[3, home, :] * lax.rsqrt(born_window[home, :])
    spread_columns(own_over, born_columns, 0)

    def energy_near(tile, carry):
        partner = [row_of(buffer, 2 * tiles + tile) for buffer in (over_window, charge_window)]
        for step in range(steps):
            rows = pl.ds(step * ROWS, ROWS)
            sums[tile, 0, rows, :] = energy_part(
                distances[tile, 0, rows, :], born_columns[tile, 0, rows, :], *partner
            )
        return carry

    lax.fori_loop(0, tiles, energy_near, 0, unroll=4)
    wait_all(born_window, born_send, born_recv)
    over_window[...] = 1.0 / born_window[...]
    charge_window[...] = window[3] * lax.rsqrt(born_window[...])

    def energy_gather(tile, carry):
        for entry in range(1, width):
            index = lists[entry, tile]
            partners[tile, entry, 0] = row_of(over_window, index)
            partners[tile, entry, 1] = jnp.where(
                entry < counts[tile], row_of(charge_window, index), 0.0
            )
        return carry

    lax.fori_loop(0, tiles, energy_gather, 0, unroll=4)

    def energy_far(tile, carry):
        def one_step(step, inner):
            rows = pl.ds(pl.multiple_of(step * ROWS, ROWS), ROWS)
            own_column = born_columns[tile, 0, rows, :]
            total = sums[tile, 0, rows, :]
            for entry in range(1, width):
                total = total + energy_part(
                    distances[tile, entry, rows, :],
                    own_column,
                    partners[tile, entry, 0],
                    partners[tile, entry, 1],
                )
            sums[tile, 0, rows, :] = total
            return inner

        lax.fori_loop(0, steps, one_step, 0, unroll=steps)
        return carry

    lax.fori_loop(0, tiles, energy_far, 0, unroll=4)

    energy = -0.5 * charge_window[home, :] * row_sums()
    energy_out[...] = energy
    total_window[pl.ds(me, 1), :] = jnp.sum(energy, axis=0, keepdims=True)

    def total_copy(step):
        mine = total_window.at[pl.ds(me, 1), :]
        return pltpu.make_async_remote_copy(
            src_ref=mine,
            dst_ref=mine,
            send_sem=total_send.at[step],
            recv_sem=total_recv.at[step],
            device_id=(lax.rem(me + step, count),),
            device_id_type=MESH,
        )

    def total_start(step, carry):
        total_copy(step).start()
        return carry

    def total_wait(step, carry):
        total_copy(step).wait_recv()
        return carry

    def total_sent(step, carry):
        total_copy(step).wait_send()
        return carry

    lax.fori_loop(1, count, total_start, 0)
    lax.fori_loop(1, count, total_wait, 0)
    total_out[0, 0] = jnp.sum(total_window[...])
    lax.fori_loop(1, count, total_sent, 0)


def hand_over(born, energy, born_out, energy_out):
    born_out[...] = born[...]
    energy_out[...] = energy[...]


def solution(mesh):
    count = mesh.shape["slab"]

    def shards(coords, charges, radii, screens, tile_lists, tile_counts, slab_fill):
        tiles = charges.shape[0] // LANES
        width = tile_lists.shape[1]
        block = jax.ShapeDtypeStruct((tiles, LANES), jnp.float32)
        smem = pl.BlockSpec(memory_space=pltpu.SMEM)
        hbm = pl.BlockSpec(memory_space=pltpu.HBM)
        vmem = pl.BlockSpec(memory_space=pltpu.VMEM)
        born, energy, total = pl.pallas_call(
            functools.partial(kernel, count),
            out_shape=(block, block, jax.ShapeDtypeStruct((1, 1), jnp.float32)),
            in_specs=[hbm] * 7,
            out_specs=(vmem, vmem, smem),
            scratch_shapes=[
                pltpu.SMEM((width, tiles), jnp.int32),
                pltpu.SMEM((tiles,), jnp.int32),
                pltpu.SMEM((1,), jnp.int32),
                pltpu.VMEM(coords.shape, jnp.float32),
                pltpu.VMEM((tiles, LANES), jnp.float32),
                pltpu.VMEM((tiles, LANES), jnp.float32),
                pltpu.VMEM((tiles, LANES), jnp.float32),
                pltpu.VMEM((5, 5 * tiles, LANES), jnp.float32),
                pltpu.VMEM((5 * tiles, LANES), jnp.float32),
                pltpu.VMEM((5 * tiles, LANES), jnp.float32),
                pltpu.VMEM((5 * tiles, LANES), jnp.float32),
                pltpu.VMEM((count, LANES), jnp.float32),
                pltpu.VMEM((tiles, 4, LANES, LANES), jnp.float32),
                pltpu.VMEM((tiles, 1, LANES, LANES), jnp.float32),
                pltpu.VMEM((tiles, width, 5, ROWS, LANES), jnp.float32),
                pltpu.VMEM((tiles, 3, LANES, LANES), jnp.float32),
                pltpu.VMEM((tiles, width, LANES, LANES), jnp.float32),
                pltpu.SemaphoreType.DMA((7,)),
                pltpu.SemaphoreType.DMA((len(SHIFTS),)),
                pltpu.SemaphoreType.DMA((len(SHIFTS),)),
                pltpu.SemaphoreType.DMA((len(SHIFTS),)),
                pltpu.SemaphoreType.DMA((len(SHIFTS),)),
                pltpu.SemaphoreType.DMA((count,)),
                pltpu.SemaphoreType.DMA((count,)),
            ],
            compiler_params=pltpu.CompilerParams(
                collective_id=0, has_side_effects=True, vmem_limit_bytes=63463424

            ),
        )(
            tile_lists.T,
            tile_counts,
            slab_fill,
            coords,
            charges.reshape(tiles, LANES),
            radii.reshape(tiles, LANES),
            screens.reshape(tiles, LANES),
        )
        born, energy = pl.pallas_call(
            hand_over,
            out_shape=(block, block),
            in_specs=[vmem] * 2,
            out_specs=(vmem, vmem),
        )(born, energy)
        return born.reshape(-1), energy.reshape(-1), total.reshape(())

    placed = (
        P(None, "slab"),
        P("slab"),
        P("slab"),
        P("slab"),
        P("slab", None),
        P("slab"),
        P("slab"),
    )
    return jax.shard_map(
        shards, mesh=mesh, in_specs=placed, out_specs=(P("slab"), P("slab"), P()), check_vma=False
    )
```
